32 devices in a mesh: groups: 1, pool: 16 (over z, y, core), head: 2 (over x), sub: 1.
Axes of the slice: x: 2, y: 2, z: 4, core: 2. Of those that a mesh axis runs over, the one named last changes fastest.
Arguments:
- queries: bfloat16 [4096, 36864], P(('groups', 'pool'), ('head', 'sub')), may hold values from -64 to 64, as said below
- pool_cache: bfloat16 [64, 36864], P(('groups', 'pool')), may hold values from -5 to 5
- new_blocks: bfloat16 [64, 36864], P(('groups', 'pool')), may hold values from -5 to 5, as said below
- w_uv: bfloat16 [64, 512, 128], P(('head', 'sub')), may hold values from -0.25 to 0.25
- owners: int32 [64, 8, 1], P('groups'), may hold values from 0 to 15; in each aligned block of 32 rows (0 to 31, 32 to 63, ..., all dimensions but the last counted through in order) at most 4 rows name the same one
- slots: int32 [64, 8], P('groups'), may hold values from 0 to 3
- prefix_len: int32 [64], P('groups'), may hold values from 1 to 512, 16384 in all
- new_len: int32 [64], P('groups'), may hold values from 1 to 64, 3072 in all
- dest: int32 [64, 1], P('groups'), may hold values from 0 to 15; in each aligned block of 4 rows (0 to 3, 4 to 7, ...) no two rows name the same one
Outputs:
- attn_out: bfloat16 [4096, 8192], P(('groups', 'pool'), ('head', 'sub'))
- decode_cache: bfloat16 [256, 36864], P(('groups', 'pool'), ('head', 'sub'))
The draws below stay inside these ranges and needn't reach their ends.
Inputs may be any that keep to these rules, and one draw needn't show every extreme that they name: `queries`: custom draw. `new_blocks`: custom draw. `owners`: the 32 list entries of the requests of one pool device name no pool device more than 4 times; some pool device's entries name some device exactly 4 times. `prefix_len`: the longest prefix is exactly 512 tokens. `new_len`: some request has exactly 64 new tokens. `dest`: the 4 requests of one pool device go to 4 different decode groups.
All inputs are finite; a program needn't handle non-finite values.
Results may differ from the reference program's by a relative error of at most 0.0051.
Values may be sent and summed in bfloat16 or wider, within the bound.
A program may use at most 128 MiB of HBM per device.

```python
import math
import jax
import jax.numpy as jnp
import numpy as np
from jax import lax

KVL = 512
LAT = 576
VH = 128
H = 64
BLK = 64
C = 64
MAXB = 8
POOL_DEV = 4
REQ_DEV = 4
PAIRCAP = 4
REQS = 64
CB = 1
N_POOL = 16


def draw_queries(key, part):
    key = jax.random.fold_in(key, 11)
    key_base = jax.random.fold_in(key, 0)
    values = 1.25 * jnp.clip(jax.random.normal(key_base, (REQS * C, H, LAT), jnp.float32), -5.0, 5.0)
    return values.reshape(REQS * C, H * LAT).astype(jnp.bfloat16)


def draw_new_blocks(key, part):
    key = jax.random.fold_in(key, 23)
    values = jnp.clip(jax.random.normal(key, (REQS, C, LAT), jnp.float32), -5.0, 5.0)
    return values.reshape(REQS * C // BLK, BLK * LAT).astype(jnp.bfloat16)


def plant(array, stream_key, low, largest):
    longest = array.shape.index(max(array.shape))
    spots = []
    for shift in (0, 1):
        where = [jax.random.randint(jax.random.fold_in(stream_key, axis), (), 0, length) for axis, length in enumerate(array.shape)]
        where[longest] = (where[longest] + shift) % array.shape[longest]
        spots.append(tuple(where))
    return array.at[spots[0]].set(low).at[spots[1]].set(largest)


def level_of(key, shape, shards, low, largest):
    def one(axis_at, parts):
        heights = jax.random.uniform(jax.random.fold_in(jax.random.fold_in(key, 6), axis_at), (parts,), jnp.float32, low / len(shards), largest / len(shards))
        return jnp.repeat(jnp.exp(heights), shape[axis_at] // parts).reshape((-1,) + (1,) * (len(shape) - axis_at - 1))

    level = one(*shards[0])
    for cut in shards[1:]:
        level = level * one(*cut)
    return level


def split_up(number_of, total, limit, lean):
    portions = [(1 << 20) // math.isqrt(grade ** lean) + 1 for grade in range(2, number_of + 1)]
    rest, given = total - limit - (number_of - 1), [1] * (number_of - 1)
    while rest > 0:
        free = [i for i in range(number_of - 1) if given[i] < limit]
        mass, left = sum([portions[i] for i in free]), rest
        for i in free:
            more = min(limit - given[i], max(1, left * portions[i] // mass), rest)
            given[i] = given[i] + more
            rest = rest - more
    return np.array([limit] + given)


def uneven_parts(stream_key, amount, total, most, skew):
    if amount == 2:
        one = jax.random.randint(stream_key, (), max(1, total - most), min(most, total - 1) + 1)
        return jnp.stack([one, total - one])
    tallies = jnp.asarray(split_up(amount, total, most, skew), jnp.int32)
    couples = (amount - 1) // 2
    source_of, receiver = tallies[1:1 + 2 * couples:2], tallies[2:2 + 2 * couples:2]
    room = jnp.minimum(source_of - 1, most - receiver)
    shifted = jax.random.randint(jax.random.fold_in(stream_key, 1), (couples,), 0, 1 << 20) % (room + 1)
    tallies = tallies.at[1:1 + 2 * couples:2].set(source_of - shifted).at[2:2 + 2 * couples:2].set(receiver + shifted)
    return tallies[jax.random.permutation(jax.random.fold_in(stream_key, 2), amount)]


def assign_block(stream_key, own, number, rows, number_of, top, bound, slope):
    ranking = jax.random.permutation(stream_key, number_of)
    packed, ordinary = load_shares(number_of, rows * top, bound, slope, True), load_shares(number_of, rows * top, bound, slope, False)
    places = jnp.arange(number_of)

    def named(lengths, offset_by):
        used = int((lengths > 0).sum())
        fixed = max(1, used // 4)
        shifted = fixed + (places - fixed + offset_by * (used - fixed)) % max(1, number_of - fixed)
        return jnp.zeros((number_of,), jnp.int32).at[ranking[jnp.where(places < fixed, places, shifted)]].set(jnp.asarray(lengths, jnp.int32))

    lengths = jnp.where(number % 4 == 0, named(packed, number // 4), named(ordinary, number - number // 4 - 1))
    mixed = jax.random.permutation(jax.random.fold_in(own, 3), number_of)
    giver, sink = mixed[0:number_of // 2 * 2:2], mixed[1:number_of // 2 * 2:2]
    margin = jnp.minimum(lengths[giver] - 1, bound - lengths[sink]) // 2
    margin = jnp.where((giver == ranking[0]) | (sink == ranking[0]) | (lengths[sink] == 0), 0, jnp.maximum(margin, 0))
    shifted = jax.random.randint(jax.random.fold_in(own, 4), (number_of // 2,), 0, 1 << 20) % (margin + 1)
    lengths = lengths.at[giver].add(-shifted).at[sink].add(shifted)
    items = jnp.searchsorted(jnp.cumsum(lengths), jnp.arange(rows * top), side="right").astype(jnp.int32)
    table = items.reshape(top, rows).T
    table = table[jax.random.permutation(jax.random.fold_in(own, 1), rows)]
    offset_by = jax.random.randint(jax.random.fold_in(own, 2), (rows, 1), 0, top)
    return jnp.take_along_axis(table, (jnp.arange(top)[None, :] + offset_by) % top, axis=1)


def load_shares(number_of, total, most, skew, full):
    weights = [(1 << 20) // math.isqrt(grade ** skew) + 1 for grade in range(1, number_of + 1)]
    largest = most if full else min(most, max(-(-total // number_of), total * weights[0] // sum(weights)))
    least = 1 if total - largest >= number_of - 1 else 0
    counts, surplus = [largest] + [least] * (number_of - 1), total - largest - least * (number_of - 1)
    while surplus > 0:
        movable = [i for i in range(1, number_of) if counts[i] < largest] or [i for i in range(1, number_of) if counts[i] < most]
        whole, budget = sum([weights[i] for i in movable]), surplus
        for i in movable:
            addition = min(most - counts[i], max(1, budget * weights[i] // whole), surplus)
            counts[i] = counts[i] + addition
            surplus = surplus - addition
    return np.array(counts)


def normal_values(stream_key, extent, deviation, bound, pieces=(), kind=jnp.bfloat16):
    level = level_of(stream_key, extent, pieces, -0.22, 0.18) if pieces else 1.0
    entries = jax.random.normal(stream_key, extent, jnp.float32) * deviation * level
    return jnp.minimum(jnp.maximum(entries, -bound), bound).astype(kind)


def setup_inputs(seed: int = 0, part: int = 0) -> dict:
    streams_of = jax.random.split(jax.random.key(seed), 10)
    own_keys = jax.random.split(jax.random.fold_in(streams_of[9], part), 10)
    queries = draw_queries(jax.random.fold_in(jax.random.fold_in(streams_of[9], part), 71), part)
    pool_cache = normal_values(own_keys[1], (N_POOL * POOL_DEV, BLK * LAT), 1.0, 5.0, ((0, 16),))
    new_blocks = draw_new_blocks(jax.random.fold_in(jax.random.fold_in(streams_of[9], part), 71), part)
    w_uv = normal_values(streams_of[3], (H, KVL, VH), KVL ** -0.5, 0.25, ((0, 2),))
    owners_keys = jax.random.split(jax.random.fold_in(own_keys[4], 1), REQS * MAXB // (REQ_DEV * MAXB))
    owners_turns = jax.random.permutation(jax.random.fold_in(own_keys[4], 3), REQS * MAXB // (REQ_DEV * MAXB))
    owners = jax.vmap(lambda own, number: assign_block(jax.random.fold_in(own_keys[4], 2), own, number, REQ_DEV * MAXB, N_POOL, 1, PAIRCAP, 2))(owners_keys, owners_turns).reshape((REQS, MAXB, 1))
    slots = plant(jax.random.randint(own_keys[5], (REQS, MAXB), 0, POOL_DEV), jax.random.fold_in(own_keys[5], 1), 0, POOL_DEV - 1).astype(jnp.int32)
    prefix_len = uneven_parts(own_keys[6], REQS, REQS * MAXB * BLK // 2, MAXB * BLK, 2).astype(jnp.int32)
    new_len = uneven_parts(own_keys[7], REQS, REQS * C * 3 // 4, C, 2).astype(jnp.int32)
    dest_keys = jax.random.split(jax.random.fold_in(own_keys[8], 1), REQS // REQ_DEV)
    dest_turns = jax.random.permutation(jax.random.fold_in(own_keys[8], 3), REQS // REQ_DEV)
    dest = jax.vmap(lambda own, number: assign_block(jax.random.fold_in(own_keys[8], 2), own, number, REQ_DEV, N_POOL, 1, 1, 2))(dest_keys, dest_turns).reshape((REQS, 1))
    return {"queries": queries, "pool_cache": pool_cache, "new_blocks": new_blocks, "w_uv": w_uv, "owners": owners, "slots": slots, "prefix_len": prefix_len, "new_len": new_len, "dest": dest}


softmax_scale = 192.0 ** -0.5
far_below = -1.0e30


def reference(queries, pool_cache, new_blocks, w_uv, owners, slots, prefix_len, new_len, dest):
    pool_rows = pool_cache.reshape(N_POOL * POOL_DEV, BLK, LAT)
    block_ids = (owners[:, :, 0] * POOL_DEV + slots).astype(jnp.int32)
    fresh_all = new_blocks.reshape(REQS, C, LAT)
    query_all = queries.reshape(REQS, C, H, LAT)
    weights_uv = w_uv.astype(jnp.float32)
    query_pos = jnp.arange(C, dtype=jnp.int32)
    prefix_pos = jnp.arange(MAXB * BLK, dtype=jnp.int32)

    def one_request(request):
        prefix = pool_rows[block_ids[request]].reshape(MAXB * BLK, LAT)
        all_keys = jnp.concatenate([prefix, fresh_all[request]], axis=0).astype(jnp.float32)
        query = query_all[request].astype(jnp.float32)
        scores = jnp.einsum("chl,kl->chk", query, all_keys) * softmax_scale
        prefix_live = jnp.broadcast_to(prefix_pos[None, :] < prefix_len[request], (C, MAXB * BLK))
        fresh_live = query_pos[None, :] <= query_pos[:, None]
        allowed = jnp.concatenate([prefix_live, fresh_live], axis=1)[:, None, :]
        scores = jnp.where(allowed, scores, far_below)
        row_max = jnp.max(scores, axis=-1, keepdims=True)
        weights = jnp.where(allowed, jnp.exp(scores - row_max), 0.0)
        row_total = jnp.sum(weights, axis=-1)
        rounded = lax.optimization_barrier(weights.astype(jnp.bfloat16)).astype(jnp.float32)
        latent_out = jnp.einsum("chk,kd->chd", rounded, all_keys[:, :KVL]) / row_total[:, :, None]
        latent_out = lax.optimization_barrier(latent_out.astype(jnp.bfloat16)).astype(jnp.float32)
        projected = jnp.einsum("chd,hdv->chv", latent_out, weights_uv)
        projected = jnp.where((query_pos < new_len[request])[:, None, None], projected, 0.0)
        return projected.astype(jnp.bfloat16).reshape(C, H * VH)

    attn_out = lax.map(one_request, jnp.arange(REQS, dtype=jnp.int32)).reshape(REQS * C, H * VH)
    dest_flat = dest[:, 0]
    live_tok = query_pos[None, :] < new_len[:, None]
    masked = jnp.where(live_tok[:, :, None], fresh_all, jnp.zeros((), fresh_all.dtype))
    sender = (jnp.arange(REQS, dtype=jnp.int32) // REQ_DEV).astype(jnp.int32)
    row_ids = (dest_flat * N_POOL + sender).astype(jnp.int32)
    slotted = jnp.zeros((N_POOL * N_POOL, C * LAT), new_blocks.dtype).at[row_ids].set(masked.reshape(REQS, C * LAT))
    decode_cache = slotted.reshape(N_POOL * N_POOL * CB, BLK * LAT)
    return attn_out, decode_cache
```

```python
import functools
import math

import jax
import jax.numpy as jnp
from jax import lax
from jax.experimental import pallas as pl
from jax.experimental.pallas import tpu as pltpu
from jax.sharding import PartitionSpec as P

KVL = 512
LAT = 576
VH = 128
BLK = 64
C = 64
MAXB = 8
POOL_DEV = 4
REQ_DEV = 4
WIN = 640
KEYS = (MAXB + 1) * BLK
TOK = 16

EXP_SCALE = 192.0 ** -0.5 * math.log2(math.e)
FAR_BELOW = -1e30


def attend_kernel(
    owners, slots, prefix_len, new_len,
    queries, gathered, fresh, w_uv, out,
    q_buf, key_buf, w_buf, keys_t, keys_v, latent, q_sem, key_sem, fresh_sem, w_sem,
):
    heads = w_uv.shape[0]
    pairs = heads // 2
    first = lax.axis_index("pool") * REQ_DEV

    def q_copy(r):
        return pltpu.make_async_copy(
            queries.at[pl.ds(r * C, C)], q_buf.at[pl.ds(r * C, C)], q_sem.at[r]
        )

    def key_copy(r, k):
        row = owners[first + r, k] * POOL_DEV + slots[first + r, k]
        return pltpu.make_async_copy(
            gathered.at[row], key_buf.at[r, pl.ds((k + 1) * BLK, BLK)], key_sem.at[r, k]
        )

    def fresh_copy(r):
        return pltpu.make_async_copy(
            fresh.at[r], key_buf.at[r, pl.ds(0, BLK)], fresh_sem.at[r]
        )

    w_copy = pltpu.make_async_copy(w_uv, w_buf, w_sem)
    for r in range(REQ_DEV):
        fresh_copy(r).start()
        for k in range(MAXB):
            key_copy(r, k).start()
        q_copy(r).start()
    w_copy.start()

    keys_t[...] = jnp.zeros_like(keys_t)
    keys_v[pl.ds(KEYS, WIN - KEYS), :] = jnp.zeros((WIN - KEYS, KVL), jnp.bfloat16)

    def run(r, width, plen, nlen):
        def chunk(i, carry):
            tok = pl.multiple_of(i * TOK, TOK)
            row = pl.multiple_of(r * C + tok, TOK)
            col = lax.broadcasted_iota(jnp.int32, (TOK, width), 1)
            pos = lax.broadcasted_iota(jnp.int32, (TOK, width), 0) + tok
            last = jnp.where(col < BLK, pos, plen + BLK - 1)
            bias = jnp.where(col <= last, 0.0, FAR_BELOW)
            for parity in range(2):
                shift = parity * KVL
                q = jnp.concatenate(
                    [q_buf[pl.ds(row, TOK), pl.ds(g * 2 * LAT + shift, WIN)] for g in range(pairs)], axis=0
                )
                s = jnp.dot(q, keys_t[parity, :, :width], preferred_element_type=jnp.float32)
                s = (s.reshape(pairs, TOK, width) + bias[None]).reshape(pairs * TOK, width)
                top = jnp.max(s, axis=1, keepdims=True)
                p = jnp.exp2((s - top) * EXP_SCALE)
                total = jnp.sum(p, axis=1, keepdims=True)
                o = jnp.dot(p.astype(jnp.bfloat16), keys_v[:width], preferred_element_type=jnp.float32)
                o = (o * (1.0 / total)).astype(jnp.bfloat16)
                for g in range(pairs):
                    latent[2 * g + parity, pl.ds(row, TOK), :] = o[g * TOK:(g + 1) * TOK]
            return carry

        lax.fori_loop(0, (nlen + TOK - 1) // TOK, chunk, 0)

    def request(r, carry):
        plen = prefix_len[first + r]
        nlen = new_len[first + r]
        fresh_copy(r).wait()
        for k in range(MAXB):
            key_copy(r, k).wait()
        keys = key_buf[r]
        keys_v[pl.ds(0, KEYS), :] = keys[:, :KVL]
        flipped = keys.T
        keys_t[0, pl.ds(0, LAT), pl.ds(0, KEYS)] = flipped
        keys_t[1, pl.ds(WIN - LAT, LAT), pl.ds(0, KEYS)] = flipped
        q_copy(r).wait()
        pl.when(plen <= 192)(lambda: run(r, 256, plen, nlen))
        pl.when((plen > 192) & (plen <= 448))(lambda: run(r, 512, plen, nlen))
        pl.when(plen > 448)(lambda: run(r, WIN, plen, nlen))
        return carry

    lax.fori_loop(0, REQ_DEV, request, 0)
    w_copy.wait()

    rows = REQ_DEV * C
    at = lax.broadcasted_iota(jnp.int32, (rows, VH), 0)
    live = jnp.zeros((rows, VH), jnp.int32)
    for r in range(REQ_DEV):
        live = jnp.where((at >= r * C) & (at < r * C + new_len[first + r]), 1, live)

    def project(h, carry):
        value = jnp.dot(latent[h], w_buf[h], preferred_element_type=jnp.float32)
        out[:, pl.ds(pl.multiple_of(h * VH, VH), VH)] = jnp.where(live == 1, value, 0.0).astype(out.dtype)
        return carry

    lax.fori_loop(0, heads, project, 0, unroll=4)


def attend(queries, gathered, fresh, w_uv, owners, slots, prefix_len, new_len):
    heads = w_uv.shape[0]
    rows = REQ_DEV * C
    flops = 2 * rows * heads * (KEYS * (LAT + KVL) + KVL * VH)
    return pl.pallas_call(
        attend_kernel,
        grid_spec=pltpu.PrefetchScalarGridSpec(
            num_scalar_prefetch=4,
            grid=(1,),
            in_specs=[pl.BlockSpec(memory_space=pl.ANY)] * 4,
            out_specs=pl.BlockSpec((rows, heads * VH), lambda i, *_: (0, 0)),
            scratch_shapes=[
                pltpu.VMEM((rows, heads * LAT), jnp.bfloat16),
                pltpu.VMEM((REQ_DEV, KEYS, LAT), jnp.bfloat16),
                pltpu.VMEM(w_uv.shape, jnp.bfloat16),
                pltpu.VMEM((2, WIN, WIN), jnp.bfloat16),
                pltpu.VMEM((WIN, KVL), jnp.bfloat16),
                pltpu.VMEM((heads, rows, KVL), jnp.bfloat16),
                pltpu.SemaphoreType.DMA((REQ_DEV,)),
                pltpu.SemaphoreType.DMA((REQ_DEV, MAXB)),
                pltpu.SemaphoreType.DMA((REQ_DEV,)),
                pltpu.SemaphoreType.DMA,
            ],
        ),
        out_shape=jax.ShapeDtypeStruct((rows, heads * VH), jnp.bfloat16),
        compiler_params=pltpu.CompilerParams(vmem_limit_bytes=56 * 1024 * 1024),
        cost_estimate=pl.CostEstimate(flops=flops, bytes_accessed=queries.size * 2, transcendentals=rows * heads * KEYS),
        name="attend",
    )(owners, slots, prefix_len, new_len, queries, gathered, fresh, w_uv)


def decode_rows(new_blocks, new_len, dest, own):
    pool_count = lax.axis_size("pool")
    share = new_blocks.shape[1] // lax.axis_size(("head", "sub"))
    start = lax.axis_index(("head", "sub")) * share
    part = lax.dynamic_slice_in_dim(new_blocks, start, share, 1)
    tok = (jnp.arange(share, dtype=jnp.int32) + start) // LAT
    lens = lax.dynamic_slice_in_dim(new_len, own, REQ_DEV, 0)
    goes = lax.dynamic_slice_in_dim(dest[:, 0], own, REQ_DEV, 0)
    part = jnp.where(tok[None, :] < lens[:, None], part, 0)
    rows = jnp.zeros((pool_count, share), new_blocks.dtype)
    for r in range(REQ_DEV):
        rows = jnp.where((goes[r] == jnp.arange(pool_count))[:, None], part[r][None, :], rows)
    return rows.reshape(pool_count, share // 128, 128)


def body(queries, pool_cache, new_blocks, w_uv, owners, slots, prefix_len, new_len, dest):
    own = lax.axis_index("pool") * REQ_DEV
    blocks = pool_cache.reshape(POOL_DEV, BLK, LAT)
    fresh = new_blocks.reshape(REQ_DEV, C, LAT)
    gathered = lax.all_gather(blocks, "pool", axis=0, tiled=True)
    leaving = decode_rows(new_blocks, new_len, dest, own)
    gathered, leaving = lax.optimization_barrier((gathered, leaving))
    arrived = lax.all_to_all(leaving, "pool", split_axis=0, concat_axis=0, tiled=True)
    attn_out = attend(queries, gathered, fresh, w_uv, owners[:, :, 0], slots, prefix_len, new_len)
    decode_cache = arrived.reshape(arrived.shape[0], -1)
    return attn_out, decode_cache


def solution(mesh):
    placed = (
        P(("groups", "pool"), ("head", "sub")),
        P(("groups", "pool"), None),
        P(("groups", "pool"), None),
        P(("head", "sub"), None, None),
        P("groups", None, None),
        P("groups", None),
        P("groups"),
        P("groups"),
        P("groups", None),
    )
    return jax.shard_map(
        body,
        mesh=mesh,
        in_specs=placed,
        out_specs=(P(("groups", "pool"), ("head", "sub")), P(("groups", "pool"), ("head", "sub"))),
        check_vma=False,
    )
```

```python
import functools
import math

import jax
import jax.numpy as jnp
from jax import lax
from jax.experimental import pallas as pl
from jax.experimental.pallas import tpu as pltpu
from jax.sharding import PartitionSpec as P

KVL = 512
LAT = 576
VH = 128
BLK = 64
C = 64
MAXB = 8
POOL_DEV = 4
REQ_DEV = 4
WIN = 640
KEYS = (MAXB + 1) * BLK
TOK = 16

EXP_SCALE = 192.0 ** -0.5 * math.log2(math.e)
FAR_BELOW = -1e30


def attend_kernel(
    owners, slots, prefix_len, new_len,
    queries, gathered, fresh, w_uv, out,
    q_buf, key_buf, w_buf, keys_t, keys_v, latent, q_sem, key_sem, fresh_sem, w_sem,
):
    heads = w_uv.shape[0]
    pairs = heads // 2
    first = lax.axis_index("pool") * REQ_DEV

    def q_copy(r):
        return pltpu.make_async_copy(
            queries.at[pl.ds(r * C, C)], q_buf.at[pl.ds(r * C, C)], q_sem.at[r]
        )

    def key_copy(r, k):
        row = owners[k, first + r] * POOL_DEV + slots[k, first + r]
        return pltpu.make_async_copy(
            gathered.at[row], key_buf.at[r, pl.ds((k + 1) * BLK, BLK)], key_sem.at[r, k]
        )

    def fresh_copy(r):
        return pltpu.make_async_copy(
            fresh.at[r], key_buf.at[r, pl.ds(0, BLK)], fresh_sem.at[r]
        )

    w_copy = pltpu.make_async_copy(w_uv, w_buf, w_sem)
    for r in range(REQ_DEV):
        fresh_copy(r).start()
        for k in range(MAXB):
            key_copy(r, k).start()
        q_copy(r).start()
    w_copy.start()

    keys_t[...] = jnp.zeros_like(keys_t)
    keys_v[pl.ds(KEYS, WIN - KEYS), :] = jnp.zeros((WIN - KEYS, KVL), jnp.bfloat16)

    def run(r, width, plen, nlen):
        def chunk(i, carry):
            tok = pl.multiple_of(i * TOK, TOK)
            row = pl.multiple_of(r * C + tok, TOK)
            col = lax.broadcasted_iota(jnp.int32, (TOK, width), 1)
            pos = lax.broadcasted_iota(jnp.int32, (TOK, width), 0) + tok
            last = jnp.where(col < BLK, pos, plen + BLK - 1)
            bias = jnp.where(col <= last, 0.0, FAR_BELOW)
            for parity in range(2):
                shift = parity * KVL
                q = jnp.concatenate(
                    [q_buf[pl.ds(row, TOK), pl.ds(g * 2 * LAT + shift, WIN)] for g in range(pairs)], axis=0
                )
                s = jnp.dot(q, keys_t[parity, :, :width], preferred_element_type=jnp.float32)
                s = (s.reshape(pairs, TOK, width) + bias[None]).reshape(pairs * TOK, width)
                top = jnp.max(s, axis=1, keepdims=True)
                p = jnp.exp2((s - top) * EXP_SCALE)
                total = jnp.sum(p, axis=1, keepdims=True)
                o = jnp.dot(p.astype(jnp.bfloat16), keys_v[:width], preferred_element_type=jnp.float32)
                o = (o * (1.0 / total)).astype(jnp.bfloat16)
                for g in range(pairs):
                    latent[2 * g + parity, pl.ds(row, TOK), :] = o[g * TOK:(g + 1) * TOK]
            return carry

        lax.fori_loop(0, (nlen + TOK - 1) // TOK, chunk, 0)

    def request(r, carry):
        plen = prefix_len[first + r]
        nlen = new_len[first + r]
        fresh_copy(r).wait()
        for k in range(MAXB):
            key_copy(r, k).wait()
        keys = key_buf[r]
        keys_v[pl.ds(0, KEYS), :] = keys[:, :KVL]
        flipped = keys.T
        keys_t[0, pl.ds(0, LAT), pl.ds(0, KEYS)] = flipped
        keys_t[1, pl.ds(WIN - LAT, LAT), pl.ds(0, KEYS)] = flipped
        q_copy(r).wait()
        pl.when(plen <= 192)(lambda: run(r, 256, plen, nlen))
        pl.when((plen > 192) & (plen <= 448))(lambda: run(r, 512, plen, nlen))
        pl.when(plen > 448)(lambda: run(r, WIN, plen, nlen))
        return carry

    lax.fori_loop(0, REQ_DEV, request, 0)
    w_copy.wait()

    rows = REQ_DEV * C
    at = lax.broadcasted_iota(jnp.int32, (rows, VH), 0)
    live = jnp.zeros((rows, VH), jnp.int32)
    for r in range(REQ_DEV):
        live = jnp.where((at >= r * C) & (at < r * C + new_len[first + r]), 1, live)

    def project(h, carry):
        value = jnp.dot(latent[h], w_buf[h], preferred_element_type=jnp.float32)
        out[:, pl.ds(pl.multiple_of(h * VH, VH), VH)] = jnp.where(live == 1, value, 0.0).astype(out.dtype)
        return carry

    lax.fori_loop(0, heads, project, 0, unroll=4)


def attend(queries, gathered, fresh, w_uv, owners, slots, prefix_len, new_len):
    heads = w_uv.shape[0]
    rows = REQ_DEV * C
    flops = 2 * rows * heads * (KEYS * (LAT + KVL) + KVL * VH)
    return pl.pallas_call(
        attend_kernel,
        grid_spec=pltpu.PrefetchScalarGridSpec(
            num_scalar_prefetch=4,
            grid=(1,),
            in_specs=[pl.BlockSpec(memory_space=pl.ANY)] * 4,
            out_specs=pl.BlockSpec((rows, heads * VH), lambda i, *_: (0, 0)),
            scratch_shapes=[
                pltpu.VMEM((rows, heads * LAT), jnp.bfloat16),
                pltpu.VMEM((REQ_DEV, KEYS, LAT), jnp.bfloat16),
                pltpu.VMEM(w_uv.shape, jnp.bfloat16),
                pltpu.VMEM((2, WIN, WIN), jnp.bfloat16),
                pltpu.VMEM((WIN, KVL), jnp.bfloat16),
                pltpu.VMEM((heads, rows, KVL), jnp.bfloat16),
                pltpu.SemaphoreType.DMA((REQ_DEV,)),
                pltpu.SemaphoreType.DMA((REQ_DEV, MAXB)),
                pltpu.SemaphoreType.DMA((REQ_DEV,)),
                pltpu.SemaphoreType.DMA,
            ],
        ),
        out_shape=jax.ShapeDtypeStruct((rows, heads * VH), jnp.bfloat16),
        compiler_params=pltpu.CompilerParams(vmem_limit_bytes=56 * 1024 * 1024),
        cost_estimate=pl.CostEstimate(flops=flops, bytes_accessed=queries.size * 2, transcendentals=rows * heads * KEYS),
        name="attend",
    )(owners, slots, prefix_len, new_len, queries, gathered, fresh, w_uv)


def gather_kernel(goes, lens, blocks, flat, out, leaving, own_sem, z_send, z_recv, y_send, y_recv, x_send, x_recv, c_send, c_recv):
    me = lax.axis_index("pool")
    x = lax.axis_index("head")
    z, y, c = me // 4, (me // 2) % 2, me % 2

    def group(zz, yy, cc):
        return zz * 4 + yy * 2 + cc

    below, above = {"pool": me - 4}, {"pool": me + 4}
    beside, across, sibling = {"pool": group(z, 1 - y, c)}, {"head": 1 - x}, {"pool": group(z, y, 1 - c)}

    barrier = pltpu.get_barrier_semaphore()

    def greet(device):
        pl.semaphore_signal(barrier, inc=1, device_id=device, device_id_type=pl.DeviceIdType.MESH)

    for device in (beside, across, sibling):
        greet(device)
    pl.when(z > 0)(lambda: greet(below))
    pl.when(z < 3)(lambda: greet(above))
    inner = (z > 0) & (z < 3)
    pl.when(inner)(lambda: pl.semaphore_wait(barrier, 5))
    pl.when(jnp.logical_not(inner))(lambda: pl.semaphore_wait(barrier, 4))

    def part(ref, g, half):
        return ref.at[g, pl.ds(2 * half, 2)]

    def copy(g, half, send, recv, device, own=False):
        src = blocks.at[pl.ds(2 * half, 2)] if own else part(out, g, half)
        return pltpu.make_async_remote_copy(
            src_ref=src, dst_ref=part(out, g, half), send_sem=send, recv_sem=recv,
            device_id=device, device_id_type=pl.DeviceIdType.MESH,
        )

    def real(half):
        return half + x - 2 * half * x

    def z_copy(zz, half, up, own=False):
        return copy(group(zz, y, c), real(half), z_send.at[up, zz, half], z_recv.at[zz, half], above if up else below, own)

    def y_copy(zz, yy, own=False):
        return copy(group(zz, yy, c), real(0), y_send.at[zz], y_recv.at[zz], beside, own)

    def x_copy(zz, yy, half):
        return copy(group(zz, yy, c), real(half), x_send.at[zz], x_recv.at[zz], across)

    def c_copy(zz, yy, cc, half, own=False):
        return copy(group(zz, yy, cc), real(half), c_send.at[zz, yy, half], c_recv.at[zz, yy, half], sibling, own)

    def each(distance, act):
        if distance == 0:
            act(z, None)
        else:
            pl.when(z + distance <= 3)(lambda: act(z + distance, False))
            pl.when(z - distance >= 0)(lambda: act(z - distance, True))

    def z_round(distance):
        own = distance == 0

        for half in range(2):
            def line(zz, up, half=half):
                if not own:
                    z_copy(zz, half, up).wait_recv()
                if up is None or up:
                    pl.when(z < 3)(lambda: z_copy(zz, half, 1, own).start())
                if up is None or not up:
                    pl.when(z > 0)(lambda: z_copy(zz, half, 0, own).start())
                if half == 0:
                    y_copy(zz, y, own).start()
                c_copy(zz, y, c, half, own).start()

            each(distance, line)

    def y_round(distance):
        def side(zz, up):
            y_copy(zz, 1 - y).wait_recv()
            x_copy(zz, 1 - y, 0).start()
            c_copy(zz, 1 - y, c, 0).start()

        each(distance, side)

    def x_round(distance):
        def side(zz, up):
            x_copy(zz, 1 - y, 1).wait_recv()
            c_copy(zz, 1 - y, c, 1).start()

        each(distance, side)

    z_round(0)
    own_copy = pltpu.make_async_copy(blocks, out.at[me], own_sem)
    own_copy.start()

    span = leaving.shape[1]
    start = pl.multiple_of(x * span, span)
    place = (lax.broadcasted_iota(jnp.int32, (span, 128), 0) + start) * 128 + lax.broadcasted_iota(jnp.int32, (span, 128), 1)
    rows = []
    for r in range(REQ_DEV):
        value = flat[r, pl.ds(start, span), :].astype(jnp.float32)
        target = jnp.full((span, 128), goes[me * REQ_DEV + r], jnp.int32)
        rows.append((target, jnp.where(place < lens[me * REQ_DEV + r] * LAT, value, 0.0)))
    for n in range(leaving.shape[0]):
        row = jnp.zeros((span, 128), jnp.float32)
        for target, value in rows:
            row = jnp.where(target == n, value, row)
        leaving[n] = row.astype(leaving.dtype)

    z_round(1)
    y_round(0)
    z_round(2)
    x_round(0)
    y_round(1)
    z_round(3)
    x_round(1)
    y_round(2)
    x_round(2)
    y_round(3)
    x_round(3)

    own_copy.wait()
    for zz in range(4):
        for yy in range(2):
            for half in range(2):
                c_copy(zz, yy, 1 - c, half).wait_recv()

    for zz in range(4):
        for half in range(2):
            pl.when((z < 3) & (zz <= z))(lambda zz=zz, half=half: z_copy(zz, half, 1).wait_send())
            pl.when((z > 0) & (zz >= z))(lambda zz=zz, half=half: z_copy(zz, half, 0).wait_send())
            for yy in range(2):
                c_copy(zz, yy, c, half).wait_send()
        y_copy(zz, y).wait_send()
        x_copy(zz, 1 - y, 0).wait_send()


def gather_pool(blocks, flat, dest, new_len):
    pool_count = lax.axis_size("pool")
    span = flat.shape[1] // lax.axis_size("head")
    dma = pltpu.SemaphoreType.DMA
    return pl.pallas_call(
        gather_kernel,
        out_shape=(
            jax.ShapeDtypeStruct((pool_count,) + blocks.shape, blocks.dtype),
            jax.ShapeDtypeStruct((pool_count, span, 128), flat.dtype),
        ),
        in_specs=[
            pl.BlockSpec(memory_space=pltpu.SMEM),
            pl.BlockSpec(memory_space=pltpu.SMEM),
            pl.BlockSpec(memory_space=pl.ANY),
            pl.BlockSpec(memory_space=pltpu.VMEM),
        ],
        out_specs=(pl.BlockSpec(memory_space=pl.ANY), pl.BlockSpec(memory_space=pltpu.VMEM)),
        scratch_shapes=[
            dma,
            dma((2, 4, 2)), dma((4, 2)), dma((4,)), dma((4,)), dma((4,)), dma((4,)), dma((4, 2, 2)), dma((4, 2, 2)),
        ],
        compiler_params=pltpu.CompilerParams(
            collective_id=0, has_side_effects=True, vmem_limit_bytes=56 * 1024 * 1024
        ),
        name="gather_pool",
    )(dest, new_len, blocks, flat)


def decode_rows(new_blocks, new_len, dest, own):
    pool_count = lax.axis_size("pool")
    share = new_blocks.shape[1] // lax.axis_size(("head", "sub"))
    start = lax.axis_index(("head", "sub")) * share
    part = lax.dynamic_slice_in_dim(new_blocks, start, share, 1)
    tok = (jnp.arange(share, dtype=jnp.int32) + start) // LAT
    lens = lax.dynamic_slice_in_dim(new_len, own, REQ_DEV, 0)
    goes = lax.dynamic_slice_in_dim(dest[:, 0], own, REQ_DEV, 0)
    part = jnp.where(tok[None, :] < lens[:, None], part, 0)
    rows = jnp.zeros((pool_count, share), new_blocks.dtype)
    for r in range(REQ_DEV):
        rows = jnp.where((goes[r] == jnp.arange(pool_count))[:, None], part[r][None, :], rows)
    return rows.reshape(pool_count, share // 128, 128)


def body(queries, pool_cache, new_blocks, w_uv, owners, slots, prefix_len, new_len, dest):
    own = lax.axis_index("pool") * REQ_DEV
    blocks = pool_cache.reshape(POOL_DEV, BLK, LAT)
    fresh = new_blocks.reshape(REQ_DEV, C, LAT)
    sizes = tuple(lax.axis_size(name) for name in ("groups", "pool", "head", "sub"))
    if sizes == (1, 16, 2, 1):
        flat = new_blocks.reshape(REQ_DEV, C * LAT // 128, 128)
        gathered, leaving = gather_pool(blocks, flat, dest[:, 0], new_len)
        gathered = gathered.reshape(-1, BLK, LAT)
    else:
        gathered = lax.all_gather(blocks, "pool", axis=0, tiled=True)
        leaving = decode_rows(new_blocks, new_len, dest, own)
        gathered, leaving = lax.optimization_barrier((gathered, leaving))
    arrived = lax.all_to_all(leaving, "pool", split_axis=0, concat_axis=0, tiled=True)
    attn_out = attend(queries, gathered, fresh, w_uv, owners[:, :, 0].T, slots.T, prefix_len, new_len)
    decode_cache = arrived.reshape(arrived.shape[0], -1)
    return attn_out, decode_cache


def solution(mesh):
    placed = (
        P(("groups", "pool"), ("head", "sub")),
        P(("groups", "pool"), None),
        P(("groups", "pool"), None),
        P(("head", "sub"), None, None),
        P("groups", None, None),
        P("groups", None),
        P("groups"),
        P("groups"),
        P("groups", None),
    )
    return jax.shard_map(
        body,
        mesh=mesh,
        in_specs=placed,
        out_specs=(P(("groups", "pool"), ("head", "sub")), P(("groups", "pool"), ("head", "sub"))),
        check_vma=False,
    )
```

```python
import functools
import math

import jax
import jax.numpy as jnp
from jax import lax
from jax.experimental import pallas as pl
from jax.experimental.pallas import tpu as pltpu
from jax.sharding import PartitionSpec as P

KVL = 512
LAT = 576
VH = 128
BLK = 64
C = 64
MAXB = 8
POOL_DEV = 4
REQ_DEV = 4
WIN = 640
KEYS = (MAXB + 1) * BLK
TOK = 32
PACK = BLK * LAT // 128
TILES = KVL // 128

EXP_SCALE = 192.0 ** -0.5 * math.log2(math.e)
FAR_BELOW = -1e30


def attend_kernel(
    owners, slots, prefix_len, new_len,
    queries, gathered, fresh, w_uv, out,
    q_buf, key_buf, fresh_buf, w_buf, keys_t, keys_v, rope, latent, q_sem, key_sem, fresh_sem, w_sem,
):
    heads = w_uv.shape[0]
    pairs = heads // 2
    first = lax.axis_index("pool") * REQ_DEV

    def q_copy(r):
        return pltpu.make_async_copy(
            queries.at[pl.ds(r * C, C)], q_buf.at[pl.ds(r * C, C)], q_sem.at[r]
        )

    def key_copy(r, k):
        row = owners[k, first + r] * POOL_DEV + slots[k, first + r]
        return pltpu.make_async_copy(
            gathered.at[row], key_buf.at[r, k], key_sem.at[r, k]
        )

    def fresh_copy(r):
        return pltpu.make_async_copy(
            fresh.at[r], fresh_buf.at[r], fresh_sem.at[r]
        )

    w_copy = pltpu.make_async_copy(w_uv, w_buf, w_sem)
    for r in range(REQ_DEV):
        fresh_copy(r).start()
        for k in range(MAXB):
            key_copy(r, k).start()
        q_copy(r).start()
    w_copy.start()

    keys_t[...] = jnp.zeros_like(keys_t)
    keys_v[pl.ds(KEYS, WIN - KEYS), :] = jnp.zeros((WIN - KEYS, KVL), jnp.bfloat16)

    def run(r, width, plen, nlen):
        def chunk(i, carry):
            tok = pl.multiple_of(i * TOK, TOK)
            row = pl.multiple_of(r * C + tok, TOK)
            col = lax.broadcasted_iota(jnp.int32, (TOK, width), 1)
            pos = lax.broadcasted_iota(jnp.int32, (TOK, width), 0) + tok
            last = jnp.where(col < BLK, pos, plen + BLK - 1)
            bias = jnp.where(col <= last, 0.0, FAR_BELOW)
            for parity in range(2):
                shift = parity * KVL
                q = jnp.concatenate(
                    [q_buf[pl.ds(row, TOK), pl.ds(g * 2 * LAT + shift, WIN)] for g in range(pairs)], axis=0
                )
                s = jnp.dot(q, keys_t[parity, :, :width], preferred_element_type=jnp.float32)
                s = (s.reshape(pairs, TOK, width) + bias[None]).reshape(pairs * TOK, width)
                top = jnp.max(s, axis=1, keepdims=True)
                p = jnp.exp2((s - top) * EXP_SCALE)
                total = jnp.sum(p, axis=1, keepdims=True)
                o = jnp.dot(p.astype(jnp.bfloat16), keys_v[:width], preferred_element_type=jnp.float32)
                o = (o * (1.0 / total)).astype(jnp.bfloat16)
                for g in range(pairs):
                    latent[2 * g + parity, pl.ds(row, TOK), :] = o[g * TOK:(g + 1) * TOK]
            return carry

        lax.fori_loop(0, (nlen + TOK - 1) // TOK, chunk, 0)

    def request(r, carry):
        plen = prefix_len[first + r]
        nlen = new_len[first + r]
        fresh_copy(r).wait()
        for k in range(MAXB):
            key_copy(r, k).wait()
        own = fresh_buf[r]
        keys_v[pl.ds(0, BLK), :] = own[:, :KVL]
        rope[pl.ds(0, BLK), :] = own[:, KVL:]
        for k in range(MAXB):
            for j in range(TILES):
                keys_v[pl.ds((k + 1) * BLK, BLK), pl.ds(j * 128, 128)] = key_buf[r, k, pl.ds(j * BLK, BLK), :]
            tail = key_buf[r, k, pl.ds(TILES * BLK, BLK // 2), :]
            rope[pl.ds((k + 1) * BLK, BLK // 2), :] = tail[:, :LAT - KVL]
            rope[pl.ds((k + 1) * BLK + BLK // 2, BLK // 2), :] = tail[:, LAT - KVL:]
        flipped = keys_v[pl.ds(0, KEYS), :].T
        keys_t[0, pl.ds(0, KVL), pl.ds(0, KEYS)] = flipped
        keys_t[1, pl.ds(WIN - LAT, KVL), pl.ds(0, KEYS)] = flipped
        flipped = rope[...].T
        keys_t[0, pl.ds(KVL, LAT - KVL), pl.ds(0, KEYS)] = flipped
        keys_t[1, pl.ds(WIN - LAT + KVL, LAT - KVL), pl.ds(0, KEYS)] = flipped
        q_copy(r).wait()
        pl.when(plen <= 192)(lambda: run(r, 256, plen, nlen))
        pl.when((plen > 192) & (plen <= 448))(lambda: run(r, 512, plen, nlen))
        pl.when(plen > 448)(lambda: run(r, WIN, plen, nlen))
        return carry

    lax.fori_loop(0, REQ_DEV, request, 0)
    w_copy.wait()

    rows = REQ_DEV * C
    at = lax.broadcasted_iota(jnp.int32, (rows, VH), 0)
    live = jnp.zeros((rows, VH), jnp.int32)
    for r in range(REQ_DEV):
        live = jnp.where((at >= r * C) & (at < r * C + new_len[first + r]), 1, live)

    def project(h, carry):
        value = jnp.dot(latent[h], w_buf[h], preferred_element_type=jnp.float32)
        out[:, pl.ds(pl.multiple_of(h * VH, VH), VH)] = jnp.where(live == 1, value, 0.0).astype(out.dtype)
        return carry

    lax.fori_loop(0, heads, project, 0, unroll=4)


def attend(queries, gathered, fresh, w_uv, owners, slots, prefix_len, new_len):
    heads = w_uv.shape[0]
    rows = REQ_DEV * C
    flops = 2 * rows * heads * (KEYS * (LAT + KVL) + KVL * VH)
    return pl.pallas_call(
        attend_kernel,
        grid_spec=pltpu.PrefetchScalarGridSpec(
            num_scalar_prefetch=4,
            grid=(1,),
            in_specs=[pl.BlockSpec(memory_space=pl.ANY)] * 4,
            out_specs=pl.BlockSpec((rows, heads * VH), lambda i, *_: (0, 0)),
            scratch_shapes=[
                pltpu.VMEM((rows, heads * LAT), jnp.bfloat16),
                pltpu.VMEM((REQ_DEV, MAXB, PACK, 128), jnp.bfloat16),
                pltpu.VMEM((REQ_DEV, BLK, LAT), jnp.bfloat16),
                pltpu.VMEM(w_uv.shape, jnp.bfloat16),
                pltpu.VMEM((2, WIN, WIN), jnp.bfloat16),
                pltpu.VMEM((WIN, KVL), jnp.bfloat16),
                pltpu.VMEM((KEYS, LAT - KVL), jnp.bfloat16),
                pltpu.VMEM((heads, rows, KVL), jnp.bfloat16),
                pltpu.SemaphoreType.DMA((REQ_DEV,)),
                pltpu.SemaphoreType.DMA((REQ_DEV, MAXB)),
                pltpu.SemaphoreType.DMA((REQ_DEV,)),
                pltpu.SemaphoreType.DMA,
            ],
        ),
        out_shape=jax.ShapeDtypeStruct((rows, heads * VH), jnp.bfloat16),
        compiler_params=pltpu.CompilerParams(vmem_limit_bytes=56 * 1024 * 1024),
        cost_estimate=pl.CostEstimate(flops=flops, bytes_accessed=queries.size * 2, transcendentals=rows * heads * KEYS),
        name="attend",
    )(owners, slots, prefix_len, new_len, queries, gathered, fresh, w_uv)


def gather_kernel(
    goes, lens, blocks, flat, out, leaving, packed, own_sem,
    z_send, z_recv, y_send, y_recv, x_send, x_recv, far_send, far_recv, c_send, c_recv,
):
    me = lax.axis_index("pool")
    x = lax.axis_index("head")
    z, y, c = me // 4, (me // 2) % 2, me % 2

    def group(zz, yy, cc):
        return zz * 4 + yy * 2 + cc

    below, above = {"pool": me - 4}, {"pool": me + 4}
    beside, across, sibling = {"pool": group(z, 1 - y, c)}, {"head": 1 - x}, {"pool": group(z, y, 1 - c)}

    for b in range(POOL_DEV):
        value = blocks[b]
        for j in range(TILES):
            packed[b, pl.ds(j * BLK, BLK), :] = value[:, j * 128:(j + 1) * 128]
        packed[b, pl.ds(TILES * BLK, BLK // 2), :] = jnp.concatenate([value[:BLK // 2, KVL:], value[BLK // 2:, KVL:]], axis=1)

    barrier = pltpu.get_barrier_semaphore()

    def greet(device):
        pl.semaphore_signal(barrier, inc=1, device_id=device, device_id_type=pl.DeviceIdType.MESH)

    for device in (beside, across, sibling):
        greet(device)
    pl.when(z > 0)(lambda: greet(below))
    pl.when(z < 3)(lambda: greet(above))
    inner = (z > 0) & (z < 3)
    pl.when(inner)(lambda: pl.semaphore_wait(barrier, 5))
    pl.when(jnp.logical_not(inner))(lambda: pl.semaphore_wait(barrier, 4))

    def part(ref, g, half):
        return ref.at[g, pl.ds(2 * half, 2)]

    def copy(g, half, send, recv, device, own=False):
        src = packed.at[pl.ds(2 * half, 2)] if own else part(out, g, half)
        return pltpu.make_async_remote_copy(
            src_ref=src, dst_ref=part(out, g, half), send_sem=send, recv_sem=recv,
            device_id=device, device_id_type=pl.DeviceIdType.MESH,
        )

    def real(half):
        return half + x - 2 * half * x

    def z_copy(zz, half, up, own=False):
        return copy(group(zz, y, c), real(half), z_send.at[up, zz, half], z_recv.at[zz, half], above if up else below, own)

    def y_copy(zz, yy, own=False):
        return copy(group(zz, yy, c), real(0), y_send.at[zz], y_recv.at[zz], beside, own)

    def x_copy(zz, yy, half):
        return copy(group(zz, yy, c), real(half), x_send.at[zz], x_recv.at[zz], across)

    def far_copy(half):
        return copy(group(3 - z, y, c), real(half), far_send, far_recv, across)

    def c_copy(zz, yy, cc, half, own=False):
        return copy(group(zz, yy, cc), real(half), c_send.at[zz, yy, half], c_recv.at[zz, yy, half], sibling, own)

    def each(distance, act):
        if distance == 0:
            act(z, None)
        else:
            pl.when(z + distance <= 3)(lambda: act(z + distance, False))
            pl.when(z - distance >= 0)(lambda: act(z - distance, True))

    def z_round(distance):
        own = distance == 0

        for half in range(1 if distance == 3 else 2):
            def line(zz, up, half=half):
                if not own:
                    z_copy(zz, half, up).wait_recv()
                if distance < 2 or half == 0:
                    if up is None or up:
                        pl.when(z < 3)(lambda: z_copy(zz, half, 1, own).start())
                    if up is None or not up:
                        pl.when(z > 0)(lambda: z_copy(zz, half, 0, own).start())
                if half == 0:
                    y_copy(zz, y, own).start()
                if distance == 3:
                    far_copy(half).start()
                c_copy(zz, y, c, half, own).start()

            each(distance, line)

    def y_round(distance):
        def side(zz, up):
            y_copy(zz, 1 - y).wait_recv()
            x_copy(zz, 1 - y, 0).start()
            c_copy(zz, 1 - y, c, 0).start()

        each(distance, side)

    def x_round(distance):
        def side(zz, up):
            x_copy(zz, 1 - y, 1).wait_recv()
            c_copy(zz, 1 - y, c, 1).start()

        each(distance, side)

    z_round(0)
    own_copy = pltpu.make_async_copy(packed, out.at[me], own_sem)
    own_copy.start()

    span = leaving.shape[1]
    start = pl.multiple_of(x * span, span)
    place = (lax.broadcasted_iota(jnp.int32, (span, 128), 0) + start) * 128 + lax.broadcasted_iota(jnp.int32, (span, 128), 1)
    rows = []
    for r in range(REQ_DEV):
        value = flat[r, pl.ds(start, span), :].astype(jnp.float32)
        target = jnp.full((span, 128), goes[me * REQ_DEV + r], jnp.int32)
        rows.append((target, jnp.where(place < lens[me * REQ_DEV + r] * LAT, value, 0.0)))
    for n in range(leaving.shape[0]):
        row = jnp.zeros((span, 128), jnp.float32)
        for target, value in rows:
            row = jnp.where(target == n, value, row)
        leaving[n] = row.astype(leaving.dtype)

    z_round(1)
    y_round(0)
    z_round(2)
    x_round(0)
    y_round(1)
    z_round(3)
    x_round(1)
    y_round(2)
    x_round(2)
    y_round(3)

    def far_round():
        far_copy(1).wait_recv()
        c_copy(3 - z, y, c, 1).start()

    end = jnp.logical_not(inner)
    pl.when(end)(far_round)
    x_round(3)

    own_copy.wait()
    for zz in range(4):
        for yy in range(2):
            for half in range(2):
                c_copy(zz, yy, 1 - c, half).wait_recv()

    for zz in range(4):
        for half in range(2):
            reach = 1 if half else 3
            pl.when((z < 3) & (zz <= z) & (z - zz <= reach))(lambda zz=zz, half=half: z_copy(zz, half, 1).wait_send())
            pl.when((z > 0) & (zz >= z) & (zz - z <= reach))(lambda zz=zz, half=half: z_copy(zz, half, 0).wait_send())
            for yy in range(2):
                c_copy(zz, yy, c, half).wait_send()
        y_copy(zz, y).wait_send()
        x_copy(zz, 1 - y, 0).wait_send()
    pl.when(end)(lambda: far_copy(0).wait_send())


def gather_pool(blocks, flat, dest, new_len):
    pool_count = lax.axis_size("pool")
    span = flat.shape[1] // lax.axis_size("head")
    dma = pltpu.SemaphoreType.DMA
    return pl.pallas_call(
        gather_kernel,
        out_shape=(
            jax.ShapeDtypeStruct((pool_count, POOL_DEV, PACK, 128), blocks.dtype),
            jax.ShapeDtypeStruct((pool_count, span, 128), flat.dtype),
        ),
        in_specs=[
            pl.BlockSpec(memory_space=pltpu.SMEM),
            pl.BlockSpec(memory_space=pltpu.SMEM),
            pl.BlockSpec(memory_space=pltpu.VMEM),
            pl.BlockSpec(memory_space=pltpu.VMEM),
        ],
        out_specs=(pl.BlockSpec(memory_space=pl.ANY), pl.BlockSpec(memory_space=pltpu.VMEM)),
        scratch_shapes=[
            pltpu.VMEM((POOL_DEV, PACK, 128), blocks.dtype), dma,
            dma((2, 4, 2)), dma((4, 2)), dma((4,)), dma((4,)), dma((4,)), dma((4,)), dma, dma, dma((4, 2, 2)), dma((4, 2, 2)),
        ],
        compiler_params=pltpu.CompilerParams(
            collective_id=0, has_side_effects=True, vmem_limit_bytes=56 * 1024 * 1024
        ),
        name="gather_pool",
    )(dest, new_len, blocks, flat)


def pack_blocks(blocks):
    lanes = blocks[:, :, :KVL].reshape(-1, BLK, TILES, 128).transpose(0, 2, 1, 3).reshape(-1, TILES * BLK, 128)
    tail = jnp.concatenate([blocks[:, :BLK // 2, KVL:], blocks[:, BLK // 2:, KVL:]], axis=2)
    return jnp.concatenate([lanes, tail], axis=1)


def decode_rows(new_blocks, new_len, dest, own):
    pool_count = lax.axis_size("pool")
    share = new_blocks.shape[1] // lax.axis_size(("head", "sub"))
    start = lax.axis_index(("head", "sub")) * share
    part = lax.dynamic_slice_in_dim(new_blocks, start, share, 1)
    tok = (jnp.arange(share, dtype=jnp.int32) + start) // LAT
    lens = lax.dynamic_slice_in_dim(new_len, own, REQ_DEV, 0)
    goes = lax.dynamic_slice_in_dim(dest[:, 0], own, REQ_DEV, 0)
    part = jnp.where(tok[None, :] < lens[:, None], part, 0)
    rows = jnp.zeros((pool_count, share), new_blocks.dtype)
    for r in range(REQ_DEV):
        rows = jnp.where((goes[r] == jnp.arange(pool_count))[:, None], part[r][None, :], rows)
    return rows.reshape(pool_count, share // 128, 128)


def body(queries, pool_cache, new_blocks, w_uv, owners, slots, prefix_len, new_len, dest):
    own = lax.axis_index("pool") * REQ_DEV
    blocks = pool_cache.reshape(POOL_DEV, BLK, LAT)
    fresh = new_blocks.reshape(REQ_DEV, C, LAT)
    sizes = tuple(lax.axis_size(name) for name in ("groups", "pool", "head", "sub"))
    if sizes == (1, 16, 2, 1):
        flat = new_blocks.reshape(REQ_DEV, C * LAT // 128, 128)
        gathered, leaving = gather_pool(blocks, flat, dest[:, 0], new_len)
        gathered = gathered.reshape(-1, PACK, 128)
    else:
        gathered = lax.all_gather(pack_blocks(blocks), "pool", axis=0, tiled=True)
        leaving = decode_rows(new_blocks, new_len, dest, own)
        gathered, leaving = lax.optimization_barrier((gathered, leaving))
    arrived = lax.all_to_all(leaving, "pool", split_axis=0, concat_axis=0, tiled=True)
    attn_out = attend(queries, gathered, fresh, w_uv, owners[:, :, 0].T, slots.T, prefix_len, new_len)
    decode_cache = arrived.reshape(arrived.shape[0], -1)
    return attn_out, decode_cache


def solution(mesh):
    placed = (
        P(("groups", "pool"), ("head", "sub")),
        P(("groups", "pool"), None),
        P(("groups", "pool"), None),
        P(("head", "sub"), None, None),
        P("groups", None, None),
        P("groups", None),
        P("groups"),
        P("groups"),
        P("groups", None),
    )
    return jax.shard_map(
        body,
        mesh=mesh,
        in_specs=placed,
        out_specs=(P(("groups", "pool"), ("head", "sub")), P(("groups", "pool"), ("head", "sub"))),
        check_vma=False,
    )
```

```python
import functools
import math

import jax
import jax.numpy as jnp
from jax import lax
from jax.experimental import pallas as pl
from jax.experimental.pallas import tpu as pltpu
from jax.sharding import PartitionSpec as P

KVL = 512
LAT = 576
VH = 128
BLK = 64
C = 64
MAXB = 8
POOL_DEV = 4
REQ_DEV = 4
WIN = 640
KEYS = (MAXB + 1) * BLK
TOK = 32
PACK = BLK * LAT // 128
TILES = KVL // 128

EXP_SCALE = 192.0 ** -0.5 * math.log2(math.e)
FAR_BELOW = -1e30


def attend_kernel(
    owners, slots, prefix_len, new_len,
    queries, gathered, fresh, w_uv, out,
    q_buf, key_buf, w_buf, keys_t, keys_v, rope, latent, q_sem, key_sem, fresh_sem, w_sem,
):
    heads = w_uv.shape[0]
    pairs = heads // 2
    first = lax.axis_index("pool") * REQ_DEV

    def q_copy(r):
        return pltpu.make_async_copy(
            queries.at[pl.ds(r * C, C)], q_buf.at[pl.ds(r * C, C)], q_sem.at[r]
        )

    def key_copy(r, k):
        row = owners[k, first + r] * POOL_DEV + slots[k, first + r]
        return pltpu.make_async_copy(
            gathered.at[row], key_buf.at[r, k + 1], key_sem.at[r, k]
        )

    def fresh_copy(r):
        return pltpu.make_async_copy(
            fresh.at[r], key_buf.at[r, 0], fresh_sem.at[r]
        )

    w_copy = pltpu.make_async_copy(w_uv, w_buf, w_sem)
    for r in range(REQ_DEV):
        fresh_copy(r).start()
        for k in range(MAXB):
            key_copy(r, k).start()
        q_copy(r).start()
    w_copy.start()

    keys_t[...] = jnp.zeros_like(keys_t)
    keys_v[pl.ds(KEYS, WIN - KEYS), :] = jnp.zeros((WIN - KEYS, KVL), jnp.bfloat16)

    def run(r, width, plen, nlen):
        def chunk(i, carry):
            tok = pl.multiple_of(i * TOK, TOK)
            row = pl.multiple_of(r * C + tok, TOK)
            col = lax.broadcasted_iota(jnp.int32, (TOK, width), 1)
            pos = lax.broadcasted_iota(jnp.int32, (TOK, width), 0) + tok
            last = jnp.where(col < BLK, pos, plen + BLK - 1)
            slot = col % BLK
            token = col - slot + 2 * (slot % (BLK // 2)) + slot // (BLK // 2)
            bias = jnp.where(token <= last, 0.0, FAR_BELOW)
            for parity in range(2):
                shift = parity * KVL
                q = jnp.concatenate(
                    [q_buf[pl.ds(row, TOK), pl.ds(g * 2 * LAT + shift, WIN)] for g in range(pairs)], axis=0
                )
                s = jnp.dot(q, keys_t[parity, :, :width], preferred_element_type=jnp.float32)
                s = (s.reshape(pairs, TOK, width) + bias[None]).reshape(pairs * TOK, width)
                top = jnp.max(s, axis=1, keepdims=True)
                p = jnp.exp2((s - top) * EXP_SCALE)
                total = jnp.sum(p, axis=1, keepdims=True)
                o = jnp.dot(p.astype(jnp.bfloat16), keys_v[:width], preferred_element_type=jnp.float32)
                o = (o * (1.0 / total)).astype(jnp.bfloat16)
                for g in range(pairs):
                    latent[2 * g + parity, pl.ds(row, TOK), :] = o[g * TOK:(g + 1) * TOK]
            return carry

        lax.fori_loop(0, (nlen + TOK - 1) // TOK, chunk, 0)

    def request(r, carry):
        plen = prefix_len[first + r]
        nlen = new_len[first + r]
        fresh_copy(r).wait()
        for k in range(MAXB):
            key_copy(r, k).wait()
        for k in range(MAXB + 1):
            for j in range(TILES):
                keys_v[pl.ds(k * BLK, BLK), pl.ds(j * 128, 128)] = key_buf[r, k, pl.ds(j * BLK, BLK), :]
            tail = key_buf[r, k, pl.ds(TILES * BLK, BLK // 2), :]
            rope[pl.ds(k * BLK, BLK // 2), :] = tail[:, :LAT - KVL]
            rope[pl.ds(k * BLK + BLK // 2, BLK // 2), :] = tail[:, LAT - KVL:]
        flipped = keys_v[pl.ds(0, KEYS), :].T
        keys_t[0, pl.ds(0, KVL), pl.ds(0, KEYS)] = flipped
        keys_t[1, pl.ds(WIN - LAT, KVL), pl.ds(0, KEYS)] = flipped
        flipped = rope[...].T
        keys_t[0, pl.ds(KVL, LAT - KVL), pl.ds(0, KEYS)] = flipped
        keys_t[1, pl.ds(WIN - LAT + KVL, LAT - KVL), pl.ds(0, KEYS)] = flipped
        q_copy(r).wait()
        pl.when(plen <= 192)(lambda: run(r, 256, plen, nlen))
        pl.when((plen > 192) & (plen <= 448))(lambda: run(r, 512, plen, nlen))
        pl.when(plen > 448)(lambda: run(r, WIN, plen, nlen))
        return carry

    lax.fori_loop(0, REQ_DEV, request, 0)
    w_copy.wait()

    rows = REQ_DEV * C
    at = lax.broadcasted_iota(jnp.int32, (rows, VH), 0)
    live = jnp.zeros((rows, VH), jnp.int32)
    for r in range(REQ_DEV):
        live = jnp.where((at >= r * C) & (at < r * C + new_len[first + r]), 1, live)

    def project(h, carry):
        value = jnp.dot(latent[h], w_buf[h], preferred_element_type=jnp.float32)
        out[:, pl.ds(pl.multiple_of(h * VH, VH), VH)] = jnp.where(live == 1, value, 0.0).astype(out.dtype)
        return carry

    lax.fori_loop(0, heads, project, 0, unroll=4)


def attend(queries, gathered, fresh, w_uv, owners, slots, prefix_len, new_len):
    heads = w_uv.shape[0]
    rows = REQ_DEV * C
    flops = 2 * rows * heads * (KEYS * (LAT + KVL) + KVL * VH)
    return pl.pallas_call(
        attend_kernel,
        grid_spec=pltpu.PrefetchScalarGridSpec(
            num_scalar_prefetch=4,
            grid=(1,),
            in_specs=[pl.BlockSpec(memory_space=pl.ANY)] * 4,
            out_specs=pl.BlockSpec((rows, heads * VH), lambda i, *_: (0, 0)),
            scratch_shapes=[
                pltpu.VMEM((rows, heads * LAT), jnp.bfloat16),
                pltpu.VMEM((REQ_DEV, MAXB + 1, PACK, 128), jnp.bfloat16),
                pltpu.VMEM(w_uv.shape, jnp.bfloat16),
                pltpu.VMEM((2, WIN, WIN), jnp.bfloat16),
                pltpu.VMEM((WIN, KVL), jnp.bfloat16),
                pltpu.VMEM((KEYS, LAT - KVL), jnp.bfloat16),
                pltpu.VMEM((heads, rows, KVL), jnp.bfloat16),
                pltpu.SemaphoreType.DMA((REQ_DEV,)),
                pltpu.SemaphoreType.DMA((REQ_DEV, MAXB)),
                pltpu.SemaphoreType.DMA((REQ_DEV,)),
                pltpu.SemaphoreType.DMA,
            ],
        ),
        out_shape=jax.ShapeDtypeStruct((rows, heads * VH), jnp.bfloat16),
        compiler_params=pltpu.CompilerParams(vmem_limit_bytes=56 * 1024 * 1024),
        cost_estimate=pl.CostEstimate(flops=flops, bytes_accessed=queries.size * 2, transcendentals=rows * heads * KEYS),
        name="attend",
    )(owners, slots, prefix_len, new_len, queries, gathered, fresh, w_uv)


def gather_kernel(
    goes, lens, pool, fresh, out, leaving, fresh_out, packed, raw, own_sem,
    z_send, z_recv, y_send, y_recv, x_send, x_recv, far_send, far_recv, c_send, c_recv,
):
    me = lax.axis_index("pool")
    x = lax.axis_index("head")
    z, y, c = me // 4, (me // 2) % 2, me % 2
    lane = lax.broadcasted_iota(jnp.int32, (BLK // 2, 128), 1)

    def spread(ref):
        def step(i, carry):
            at = pl.multiple_of(i * 256, 256)
            both = jnp.concatenate([ref[:, pl.ds(at, 128)], ref[:, pl.ds(at + 128, 128)]], axis=0)
            raw[pl.ds(pl.multiple_of(i * 8, 8), 8), :] = both.astype(jnp.float32)
            return carry

        lax.fori_loop(0, PACK // 2, step, 0, unroll=8)

    def pack(ref):
        for b in range(POOL_DEV):
            nine = [raw[pl.ds(POOL_DEV * j + b, BLK // 2, stride=9 * POOL_DEV), :] for j in range(9)]
            turned = [pltpu.roll(row, 64, 1) for row in nine[4:]]
            for j in range(TILES):
                odd = jnp.where(lane < 64, turned[j], turned[j + 1])
                ref[b, pl.ds(j * BLK, BLK), :] = jnp.concatenate([nine[j], odd], axis=0).astype(ref.dtype)
            ref[b, pl.ds(TILES * BLK, BLK // 2), :] = jnp.where(lane < 64, nine[4], nine[8]).astype(ref.dtype)

    def group(zz, yy, cc):
        return zz * 4 + yy * 2 + cc

    below, above = {"pool": me - 4}, {"pool": me + 4}
    beside, across, sibling = {"pool": group(z, 1 - y, c)}, {"head": 1 - x}, {"pool": group(z, y, 1 - c)}

    barrier = pltpu.get_barrier_semaphore()

    def greet(device):
        pl.semaphore_signal(barrier, inc=1, device_id=device, device_id_type=pl.DeviceIdType.MESH)

    for device in (beside, across, sibling):
        greet(device)
    pl.when(z > 0)(lambda: greet(below))
    pl.when(z < 3)(lambda: greet(above))

    spread(pool)
    pack(packed)

    inner = (z > 0) & (z < 3)
    end = jnp.logical_not(inner)
    pl.when(inner)(lambda: pl.semaphore_wait(barrier, 5))
    pl.when(end)(lambda: pl.semaphore_wait(barrier, 4))

    def real(l):
        return l + x * (3 - 2 * l)

    def copy(g, l, send, recv, device, own=False):
        src = packed.at[real(l)] if own else out.at[g, real(l)]
        return pltpu.make_async_remote_copy(
            src_ref=src, dst_ref=out.at[g, real(l)], send_sem=send, recv_sem=recv,
            device_id=device, device_id_type=pl.DeviceIdType.MESH,
        )

    def z_copy(zz, l, up, own=False):
        return copy(group(zz, y, c), l, z_send.at[up, zz, l], z_recv.at[zz, l], above if up else below, own)

    def y_copy(zz, yy, l, own=False):
        return copy(group(zz, yy, c), l, y_send.at[zz, l], y_recv.at[zz, l], beside, own)

    def x_copy(zz, l, came=False):
        return copy(group(zz, 1 - y, c), 3 - l if came else l, x_send.at[zz, l], x_recv.at[zz, l], across)

    def far_copy(l, came=False):
        return copy(group(3 - z, y, c), 3 - l if came else l, far_send.at[l], far_recv.at[l], across)

    def c_copy(zz, yy, cc, l, own=False):
        return copy(group(zz, yy, cc), l, c_send.at[zz, yy, l], c_recv.at[zz, yy, l], sibling, own)

    def each(distance, act):
        if distance == 0:
            act(z, None)
        else:
            pl.when(z + distance <= 3)(lambda: act(z + distance, False))
            pl.when(z - distance >= 0)(lambda: act(z - distance, True))

    def z_round(distance):
        own = distance == 0
        for l in range(2 if distance == 3 else 4):
            def line(zz, up, l=l):
                if not own:
                    z_copy(zz, l, up).wait_recv()
                if distance < 2 or l < 2:
                    if up is None or up:
                        pl.when(z < 3)(lambda: z_copy(zz, l, 1, own).start())
                    if up is None or not up:
                        pl.when(z > 0)(lambda: z_copy(zz, l, 0, own).start())
                if l < 2:
                    y_copy(zz, y, l, own).start()
                if distance == 3:
                    far_copy(l).start()
                c_copy(zz, y, c, l, own).start()

            each(distance, line)

    def y_round(distance):
        for l in range(2):
            def side(zz, up, l=l):
                y_copy(zz, 1 - y, l).wait_recv()
                x_copy(zz, l).start()
                c_copy(zz, 1 - y, c, l).start()

            each(distance, side)

    def x_round(distance):
        for l in range(2):
            def side(zz, up, l=l):
                x_copy(zz, l, True).wait_recv()
                c_copy(zz, 1 - y, c, 3 - l).start()

            each(distance, side)

    z_round(0)
    own_copy = pltpu.make_async_copy(packed, out.at[me], own_sem)
    own_copy.start()

    z_round(1)
    y_round(0)

    spread(fresh)
    pack(fresh_out)
    span = leaving.shape[1]
    start = x * span
    place = (lax.broadcasted_iota(jnp.int32, (span, 128), 0) + start) * 128 + lax.broadcasted_iota(jnp.int32, (span, 128), 1)
    rows = []
    for r in range(REQ_DEV):
        value = raw[pl.ds(start * REQ_DEV + r, span, stride=REQ_DEV), :]
        target = jnp.full((span, 128), goes[me * REQ_DEV + r], jnp.int32)
        rows.append((target, jnp.where(place < lens[me * REQ_DEV + r] * LAT, value, 0.0)))
    for n in range(leaving.shape[0]):
        row = jnp.zeros((span, 128), jnp.float32)
        for target, value in rows:
            row = jnp.where(target == n, value, row)
        leaving[n] = row.astype(leaving.dtype)

    z_round(2)
    x_round(0)
    y_round(1)
    z_round(3)
    x_round(1)
    y_round(2)
    x_round(2)
    y_round(3)

    def far_round():
        for l in range(2):
            far_copy(l, True).wait_recv()
            c_copy(3 - z, y, c, 3 - l).start()

    pl.when(end)(far_round)
    x_round(3)

    own_copy.wait()
    for zz in range(4):
        for yy in range(2):
            for l in range(4):
                c_copy(zz, yy, 1 - c, l).wait_recv()

    for zz in range(4):
        for l in range(4):
            reach = 3 if l < 2 else 1
            pl.when((z < 3) & (zz <= z) & (z - zz <= reach))(lambda zz=zz, l=l: z_copy(zz, l, 1).wait_send())
            pl.when((z > 0) & (zz >= z) & (zz - z <= reach))(lambda zz=zz, l=l: z_copy(zz, l, 0).wait_send())
            for yy in range(2):
                c_copy(zz, yy, c, l).wait_send()
        for l in range(2):
            y_copy(zz, y, l).wait_send()
            x_copy(zz, l).wait_send()

    def far_sent():
        for l in range(2):
            far_copy(l).wait_send()

    pl.when(end)(far_sent)


def gather_pool(pool_cache, new_blocks, dest, new_len):
    pool_count = lax.axis_size("pool")
    span = PACK // lax.axis_size("head")
    dma = pltpu.SemaphoreType.DMA
    kind = pool_cache.dtype
    vmem, smem = pl.BlockSpec(memory_space=pltpu.VMEM), pl.BlockSpec(memory_space=pltpu.SMEM)
    return pl.pallas_call(
        gather_kernel,
        out_shape=(
            jax.ShapeDtypeStruct((pool_count, POOL_DEV, PACK, 128), kind),
            jax.ShapeDtypeStruct((pool_count, span, 128), kind),
            jax.ShapeDtypeStruct((REQ_DEV, PACK, 128), kind),
        ),
        in_specs=[smem, smem, vmem, vmem],
        out_specs=(pl.BlockSpec(memory_space=pl.ANY), vmem, vmem),
        scratch_shapes=[
            pltpu.VMEM((POOL_DEV, PACK, 128), kind), pltpu.VMEM((POOL_DEV * PACK, 128), jnp.float32), dma,
            dma((2, 4, 4)), dma((4, 4)), dma((4, 2)), dma((4, 2)), dma((4, 2)), dma((4, 2)), dma((2,)), dma((2,)),
            dma((4, 2, 4)), dma((4, 2, 4)),
        ],
        compiler_params=pltpu.CompilerParams(
            collective_id=0, has_side_effects=True, vmem_limit_bytes=56 * 1024 * 1024
        ),
        name="gather_pool",
    )(dest, new_len, pool_cache, new_blocks)


def pack_blocks(blocks):
    blocks = blocks.reshape(-1, BLK // 2, 2, LAT).transpose(0, 2, 1, 3).reshape(-1, BLK, LAT)
    lanes = blocks[:, :, :KVL].reshape(-1, BLK, TILES, 128).transpose(0, 2, 1, 3).reshape(-1, TILES * BLK, 128)
    tail = jnp.concatenate([blocks[:, :BLK // 2, KVL:], blocks[:, BLK // 2:, KVL:]], axis=2)
    return jnp.concatenate([lanes, tail], axis=1)


def decode_rows(new_blocks, new_len, dest, own):
    pool_count = lax.axis_size("pool")
    share = new_blocks.shape[1] // lax.axis_size(("head", "sub"))
    start = lax.axis_index(("head", "sub")) * share
    part = lax.dynamic_slice_in_dim(new_blocks, start, share, 1)
    tok = (jnp.arange(share, dtype=jnp.int32) + start) // LAT
    lens = lax.dynamic_slice_in_dim(new_len, own, REQ_DEV, 0)
    goes = lax.dynamic_slice_in_dim(dest[:, 0], own, REQ_DEV, 0)
    part = jnp.where(tok[None, :] < lens[:, None], part, 0)
    rows = jnp.zeros((pool_count, share), new_blocks.dtype)
    for r in range(REQ_DEV):
        rows = jnp.where((goes[r] == jnp.arange(pool_count))[:, None], part[r][None, :], rows)
    return rows.reshape(pool_count, share // 128, 128)


def body(queries, pool_cache, new_blocks, w_uv, owners, slots, prefix_len, new_len, dest):
    own = lax.axis_index("pool") * REQ_DEV
    sizes = tuple(lax.axis_size(name) for name in ("groups", "pool", "head", "sub"))
    if sizes == (1, 16, 2, 1):
        gathered, leaving, fresh = gather_pool(pool_cache, new_blocks, dest[:, 0], new_len)
        gathered = gathered.reshape(-1, PACK, 128)
    else:
        gathered = lax.all_gather(pack_blocks(pool_cache), "pool", axis=0, tiled=True)
        fresh = pack_blocks(new_blocks)
        leaving = decode_rows(new_blocks, new_len, dest, own)
        gathered, leaving = lax.optimization_barrier((gathered, leaving))
    arrived = lax.all_to_all(leaving, "pool", split_axis=0, concat_axis=0, tiled=True)
    attn_out = attend(queries, gathered, fresh, w_uv, owners[:, :, 0].T, slots.T, prefix_len, new_len)
    decode_cache = arrived.reshape(arrived.shape[0], -1)
    return attn_out, decode_cache


def solution(mesh):
    placed = (
        P(("groups", "pool"), ("head", "sub")),
        P(("groups", "pool"), None),
        P(("groups", "pool"), None),
        P(("head", "sub"), None, None),
        P("groups", None, None),
        P("groups", None),
        P("groups"),
        P("groups"),
        P("groups", None),
    )
    return jax.shard_map(
        body,
        mesh=mesh,
        in_specs=placed,
        out_specs=(P(("groups", "pool"), ("head", "sub")), P(("groups", "pool"), ("head", "sub"))),
        check_vma=False,
    )
```

```python
import functools
import math

import jax
import jax.numpy as jnp
from jax import lax
from jax.experimental import pallas as pl
from jax.experimental.pallas import tpu as pltpu
from jax.sharding import PartitionSpec as P

KVL = 512
LAT = 576
VH = 128
BLK = 64
C = 64
MAXB = 8
POOL_DEV = 4
REQ_DEV = 4
WIN = 640
KEYS = (MAXB + 1) * BLK
TOK = 32
PACK = BLK * LAT // 128
TILES = KVL // 128

EXP_SCALE = 192.0 ** -0.5 * math.log2(math.e)
FAR_BELOW = -1e30


def attend_kernel(
    owners, slots, prefix_len, new_len,
    queries, gathered, fresh, w_uv, out,
    q_buf, key_buf, w_buf, keys_t, keys_v, rope, latent, q_sem, key_sem, fresh_sem, w_sem,
):
    heads = w_uv.shape[0]
    pairs = heads // 2
    first = lax.axis_index("pool") * REQ_DEV

    def q_copy(r):
        return pltpu.make_async_copy(
            queries.at[pl.ds(r * C, C)], q_buf.at[pl.ds(r * C, C)], q_sem.at[r]
        )

    def key_copy(r, k):
        row = owners[k, first + r] * POOL_DEV + slots[k, first + r]
        return pltpu.make_async_copy(
            gathered.at[row], key_buf.at[r, k + 1], key_sem.at[r, k]
        )

    def fresh_copy(r):
        return pltpu.make_async_copy(
            fresh.at[r], key_buf.at[r, 0], fresh_sem.at[r]
        )

    w_copy = pltpu.make_async_copy(w_uv, w_buf, w_sem)
    for r in range(REQ_DEV):
        fresh_copy(r).start()
        for k in range(MAXB):
            key_copy(r, k).start()
        q_copy(r).start()
    w_copy.start()

    keys_t[...] = jnp.zeros_like(keys_t)
    keys_v[pl.ds(KEYS, WIN - KEYS), :] = jnp.zeros((WIN - KEYS, KVL), jnp.bfloat16)

    def build(r, width):
        count = min(width, KEYS)
        for k in range(count // BLK):
            for j in range(TILES):
                keys_v[pl.ds(k * BLK, BLK), pl.ds(j * 128, 128)] = key_buf[r, k, pl.ds(j * BLK, BLK), :]
            tail = key_buf[r, k, pl.ds(TILES * BLK, BLK // 2), :]
            rope[pl.ds(k * BLK, BLK // 2), :] = tail[:, :LAT - KVL]
            rope[pl.ds(k * BLK + BLK // 2, BLK // 2), :] = tail[:, LAT - KVL:]
        flipped = keys_v[pl.ds(0, count), :].T
        keys_t[0, pl.ds(0, KVL), pl.ds(0, count)] = flipped
        keys_t[1, pl.ds(WIN - LAT, KVL), pl.ds(0, count)] = flipped
        flipped = rope[pl.ds(0, count), :].T
        keys_t[0, pl.ds(KVL, LAT - KVL), pl.ds(0, count)] = flipped
        keys_t[1, pl.ds(WIN - LAT + KVL, LAT - KVL), pl.ds(0, count)] = flipped

    def run(r, width, plen, nlen):
        build(r, width)

        def chunk(i, carry):
            tok = pl.multiple_of(i * TOK, TOK)
            row = pl.multiple_of(r * C + tok, TOK)
            col = lax.broadcasted_iota(jnp.int32, (TOK, width), 1)
            pos = lax.broadcasted_iota(jnp.int32, (TOK, width), 0) + tok
            last = jnp.where(col < BLK, pos, plen + BLK - 1)
            slot = col % BLK
            token = col - slot + 2 * (slot % (BLK // 2)) + slot // (BLK // 2)
            bias = jnp.where(token <= last, 0.0, FAR_BELOW)
            for parity in range(2):
                shift = parity * KVL
                q = jnp.concatenate(
                    [q_buf[pl.ds(row, TOK), pl.ds(g * 2 * LAT + shift, WIN)] for g in range(pairs)], axis=0
                )
                s = jnp.dot(q, keys_t[parity, :, :width], preferred_element_type=jnp.float32)
                s = (s.reshape(pairs, TOK, width) + bias[None]).reshape(pairs * TOK, width)
                top = jnp.max(s, axis=1, keepdims=True)
                p = jnp.exp2((s - top) * EXP_SCALE)
                total = jnp.sum(p, axis=1, keepdims=True)
                o = jnp.dot(p.astype(jnp.bfloat16), keys_v[:width], preferred_element_type=jnp.float32)
                o = (o * (1.0 / total)).astype(jnp.bfloat16)
                for g in range(pairs):
                    latent[2 * g + parity, pl.ds(row, TOK), :] = o[g * TOK:(g + 1) * TOK]
            return carry

        lax.fori_loop(0, (nlen + TOK - 1) // TOK, chunk, 0)

    def request(r, carry):
        plen = prefix_len[first + r]
        nlen = new_len[first + r]
        fresh_copy(r).wait()
        for k in range(MAXB):
            key_copy(r, k).wait()
        q_copy(r).wait()
        pl.when(plen <= 192)(lambda: run(r, 256, plen, nlen))
        pl.when((plen > 192) & (plen <= 448))(lambda: run(r, 512, plen, nlen))
        pl.when(plen > 448)(lambda: run(r, WIN, plen, nlen))
        return carry

    lax.fori_loop(0, REQ_DEV, request, 0)
    w_copy.wait()

    rows = REQ_DEV * C
    at = lax.broadcasted_iota(jnp.int32, (rows, VH), 0)
    live = jnp.zeros((rows, VH), jnp.int32)
    for r in range(REQ_DEV):
        live = jnp.where((at >= r * C) & (at < r * C + new_len[first + r]), 1, live)

    def project(h, carry):
        value = jnp.dot(latent[h], w_buf[h], preferred_element_type=jnp.float32)
        out[:, pl.ds(pl.multiple_of(h * VH, VH), VH)] = jnp.where(live == 1, value, 0.0).astype(out.dtype)
        return carry

    lax.fori_loop(0, heads, project, 0, unroll=4)


def attend(queries, gathered, fresh, w_uv, owners, slots, prefix_len, new_len):
    heads = w_uv.shape[0]
    rows = REQ_DEV * C
    flops = 2 * rows * heads * (KEYS * (LAT + KVL) + KVL * VH)
    return pl.pallas_call(
        attend_kernel,
        grid_spec=pltpu.PrefetchScalarGridSpec(
            num_scalar_prefetch=4,
            grid=(1,),
            in_specs=[pl.BlockSpec(memory_space=pl.ANY)] * 4,
            out_specs=pl.BlockSpec((rows, heads * VH), lambda i, *_: (0, 0)),
            scratch_shapes=[
                pltpu.VMEM((rows, heads * LAT), jnp.bfloat16),
                pltpu.VMEM((REQ_DEV, MAXB + 1, PACK, 128), jnp.bfloat16),
                pltpu.VMEM(w_uv.shape, jnp.bfloat16),
                pltpu.VMEM((2, WIN, WIN), jnp.bfloat16),
                pltpu.VMEM((WIN, KVL), jnp.bfloat16),
                pltpu.VMEM((KEYS, LAT - KVL), jnp.bfloat16),
                pltpu.VMEM((heads, rows, KVL), jnp.bfloat16),
                pltpu.SemaphoreType.DMA((REQ_DEV,)),
                pltpu.SemaphoreType.DMA((REQ_DEV, MAXB)),
                pltpu.SemaphoreType.DMA((REQ_DEV,)),
                pltpu.SemaphoreType.DMA,
            ],
        ),
        out_shape=jax.ShapeDtypeStruct((rows, heads * VH), jnp.bfloat16),
        compiler_params=pltpu.CompilerParams(vmem_limit_bytes=56 * 1024 * 1024),
        cost_estimate=pl.CostEstimate(flops=flops, bytes_accessed=queries.size * 2, transcendentals=rows * heads * KEYS),
        name="attend",
    )(owners, slots, prefix_len, new_len, queries, gathered, fresh, w_uv)


def gather_kernel(
    goes, lens, pool, fresh, out, decode, fresh_out, packed, raw, leaving, own_sem, stay_sem, push_send, push_recv,
    z_send, z_recv, y_send, y_recv, x_send, x_recv, far_send, far_recv, c_send, c_recv,
):
    me = lax.axis_index("pool")
    x = lax.axis_index("head")
    z, y, c = me // 4, (me // 2) % 2, me % 2
    lane = lax.broadcasted_iota(jnp.int32, (BLK // 2, 128), 1)

    def spread(ref):
        def step(i, carry):
            at = pl.multiple_of(i * 256, 256)
            both = jnp.concatenate([ref[:, pl.ds(at, 128)], ref[:, pl.ds(at + 128, 128)]], axis=0)
            raw[pl.ds(pl.multiple_of(i * 8, 8), 8), :] = both.astype(jnp.float32)
            return carry

        lax.fori_loop(0, PACK // 2, step, 0, unroll=8)

    def pack(ref):
        for b in range(POOL_DEV):
            nine = [raw[pl.ds(POOL_DEV * j + b, BLK // 2, stride=9 * POOL_DEV), :] for j in range(9)]
            turned = [pltpu.roll(row, 64, 1) for row in nine[4:]]
            for j in range(TILES):
                odd = jnp.where(lane < 64, turned[j], turned[j + 1])
                ref[b, pl.ds(j * BLK, BLK), :] = jnp.concatenate([nine[j], odd], axis=0).astype(ref.dtype)
            ref[b, pl.ds(TILES * BLK, BLK // 2), :] = jnp.where(lane < 64, nine[4], nine[8]).astype(ref.dtype)

    def group(zz, yy, cc):
        return zz * 4 + yy * 2 + cc

    below, above = {"pool": me - 4}, {"pool": me + 4}
    beside, across, sibling = {"pool": group(z, 1 - y, c)}, {"head": 1 - x}, {"pool": group(z, y, 1 - c)}

    barrier = pltpu.get_barrier_semaphore()

    def greet(device):
        pl.semaphore_signal(barrier, inc=1, device_id=device, device_id_type=pl.DeviceIdType.MESH)

    peers = decode.shape[0]
    greet(across)
    for n in range(1, peers):
        greet({"pool": (me + n) % peers})

    spread(pool)
    pack(packed)

    inner = (z > 0) & (z < 3)
    end = jnp.logical_not(inner)
    pl.semaphore_wait(barrier, peers)

    def real(l):
        return l + x * (3 - 2 * l)

    def copy(g, l, send, recv, device, own=False):
        src = packed.at[real(l)] if own else out.at[g, real(l)]
        return pltpu.make_async_remote_copy(
            src_ref=src, dst_ref=out.at[g, real(l)], send_sem=send, recv_sem=recv,
            device_id=device, device_id_type=pl.DeviceIdType.MESH,
        )

    def z_copy(zz, l, up, own=False):
        return copy(group(zz, y, c), l, z_send.at[up, zz, l], z_recv.at[zz, l], above if up else below, own)

    def y_copy(zz, yy, l, own=False):
        return copy(group(zz, yy, c), l, y_send.at[zz, l], y_recv.at[zz, l], beside, own)

    def x_copy(zz, l, came=False):
        return copy(group(zz, 1 - y, c), 3 - l if came else l, x_send.at[zz, l], x_recv.at[zz, l], across)

    def far_copy(l, came=False):
        return copy(group(3 - z, y, c), 3 - l if came else l, far_send.at[l], far_recv.at[l], across)

    def c_copy(zz, yy, cc, l, own=False):
        return copy(group(zz, yy, cc), l, c_send.at[zz, yy, l], c_recv.at[zz, yy, l], sibling, own)

    def each(distance, act):
        if distance == 0:
            act(z, None)
        else:
            pl.when(z + distance <= 3)(lambda: act(z + distance, False))
            pl.when(z - distance >= 0)(lambda: act(z - distance, True))

    def z_round(distance):
        own = distance == 0
        for l in range(2 if distance == 3 else 4):
            def line(zz, up, l=l):
                if not own:
                    z_copy(zz, l, up).wait_recv()
                if distance < 2 or l < 2:
                    if up is None or up:
                        pl.when(z < 3)(lambda: z_copy(zz, l, 1, own).start())
                    if up is None or not up:
                        pl.when(z > 0)(lambda: z_copy(zz, l, 0, own).start())
                if l < 2:
                    y_copy(zz, y, l, own).start()
                if distance == 3:
                    far_copy(l).start()
                c_copy(zz, y, c, l, own).start()

            each(distance, line)

    def y_round(distance):
        for l in range(2):
            def side(zz, up, l=l):
                y_copy(zz, 1 - y, l).wait_recv()
                x_copy(zz, l).start()
                c_copy(zz, 1 - y, c, l).start()

            each(distance, side)

    def x_round(distance):
        for l in range(2):
            def side(zz, up, l=l):
                x_copy(zz, l, True).wait_recv()
                c_copy(zz, 1 - y, c, 3 - l).start()

            each(distance, side)

    z_round(0)
    own_copy = pltpu.make_async_copy(packed, out.at[me], own_sem)
    own_copy.start()

    spread(fresh)
    pack(fresh_out)
    span = leaving.shape[1]
    start = x * span
    place = (lax.broadcasted_iota(jnp.int32, (span, 128), 0) + start) * 128 + lax.broadcasted_iota(jnp.int32, (span, 128), 1)
    rows = []
    for r in range(REQ_DEV):
        value = raw[pl.ds(start * REQ_DEV + r, span, stride=REQ_DEV), :]
        target = jnp.full((span, 128), goes[me * REQ_DEV + r], jnp.int32)
        rows.append((target, jnp.where(place < lens[me * REQ_DEV + r] * LAT, value, 0.0)))
    for n in range(leaving.shape[0]):
        row = jnp.zeros((span, 128), jnp.float32)
        for target, value in rows:
            row = jnp.where(target == n, value, row)
        leaving[n] = row.astype(leaving.dtype)

    def push(n):
        peer = (me + n) % peers
        return pltpu.make_async_remote_copy(
            src_ref=leaving.at[peer], dst_ref=decode.at[me], send_sem=push_send.at[peer], recv_sem=push_recv.at[me],
            device_id={"pool": peer}, device_id_type=pl.DeviceIdType.MESH,
        )

    def pushed(n):
        peer = (me + n) % peers
        return pltpu.make_async_remote_copy(
            src_ref=leaving.at[peer], dst_ref=decode.at[peer], send_sem=push_send.at[peer], recv_sem=push_recv.at[peer],
            device_id={"pool": peer}, device_id_type=pl.DeviceIdType.MESH,
        )

    stay = pltpu.make_async_copy(leaving.at[me], decode.at[me], stay_sem)
    stay.start()

    z_round(1)
    y_round(0)
    z_round(2)
    for n in range(1, peers):
        push(n).start()
    x_round(0)
    y_round(1)
    z_round(3)
    x_round(1)
    y_round(2)
    x_round(2)
    y_round(3)

    def far_round():
        for l in range(2):
            far_copy(l, True).wait_recv()
            c_copy(3 - z, y, c, 3 - l).start()

    pl.when(end)(far_round)
    x_round(3)

    own_copy.wait()
    stay.wait()
    for n in range(1, peers):
        pushed(n).wait_recv()
        push(n).wait_send()
    for zz in range(4):
        for yy in range(2):
            for l in range(4):
                c_copy(zz, yy, 1 - c, l).wait_recv()

    for zz in range(4):
        for l in range(4):
            reach = 3 if l < 2 else 1
            pl.when((z < 3) & (zz <= z) & (z - zz <= reach))(lambda zz=zz, l=l: z_copy(zz, l, 1).wait_send())
            pl.when((z > 0) & (zz >= z) & (zz - z <= reach))(lambda zz=zz, l=l: z_copy(zz, l, 0).wait_send())
            for yy in range(2):
                c_copy(zz, yy, c, l).wait_send()
        for l in range(2):
            y_copy(zz, y, l).wait_send()
            x_copy(zz, l).wait_send()

    def far_sent():
        for l in range(2):
            far_copy(l).wait_send()

    pl.when(end)(far_sent)


def gather_pool(pool_cache, new_blocks, dest, new_len):
    pool_count = lax.axis_size("pool")
    span = PACK // lax.axis_size("head")
    dma = pltpu.SemaphoreType.DMA
    kind = pool_cache.dtype
    vmem, smem = pl.BlockSpec(memory_space=pltpu.VMEM), pl.BlockSpec(memory_space=pltpu.SMEM)
    return pl.pallas_call(
        gather_kernel,
        out_shape=(
            jax.ShapeDtypeStruct((pool_count, POOL_DEV, PACK, 128), kind),
            jax.ShapeDtypeStruct((pool_count, span, 128), kind),
            jax.ShapeDtypeStruct((REQ_DEV, PACK, 128), kind),
        ),
        in_specs=[smem, smem, vmem, vmem],
        out_specs=(pl.BlockSpec(memory_space=pl.ANY), pl.BlockSpec(memory_space=pl.ANY), vmem),
        scratch_shapes=[
            pltpu.VMEM((POOL_DEV, PACK, 128), kind), pltpu.VMEM((POOL_DEV * PACK, 128), jnp.float32),
            pltpu.VMEM((pool_count, span, 128), kind), dma, dma, dma((pool_count,)), dma((pool_count,)),
            dma((2, 4, 4)), dma((4, 4)), dma((4, 2)), dma((4, 2)), dma((4, 2)), dma((4, 2)), dma((2,)), dma((2,)),
            dma((4, 2, 4)), dma((4, 2, 4)),
        ],
        compiler_params=pltpu.CompilerParams(
            collective_id=0, has_side_effects=True, vmem_limit_bytes=56 * 1024 * 1024
        ),
        name="gather_pool",
    )(dest, new_len, pool_cache, new_blocks)


def pack_blocks(blocks):
    blocks = blocks.reshape(-1, BLK // 2, 2, LAT).transpose(0, 2, 1, 3).reshape(-1, BLK, LAT)
    lanes = blocks[:, :, :KVL].reshape(-1, BLK, TILES, 128).transpose(0, 2, 1, 3).reshape(-1, TILES * BLK, 128)
    tail = jnp.concatenate([blocks[:, :BLK // 2, KVL:], blocks[:, BLK // 2:, KVL:]], axis=2)
    return jnp.concatenate([lanes, tail], axis=1)


def decode_rows(new_blocks, new_len, dest, own):
    pool_count = lax.axis_size("pool")
    share = new_blocks.shape[1] // lax.axis_size(("head", "sub"))
    start = lax.axis_index(("head", "sub")) * share
    part = lax.dynamic_slice_in_dim(new_blocks, start, share, 1)
    tok = (jnp.arange(share, dtype=jnp.int32) + start) // LAT
    lens = lax.dynamic_slice_in_dim(new_len, own, REQ_DEV, 0)
    goes = lax.dynamic_slice_in_dim(dest[:, 0], own, REQ_DEV, 0)
    part = jnp.where(tok[None, :] < lens[:, None], part, 0)
    rows = jnp.zeros((pool_count, share), new_blocks.dtype)
    for r in range(REQ_DEV):
        rows = jnp.where((goes[r] == jnp.arange(pool_count))[:, None], part[r][None, :], rows)
    return rows.reshape(pool_count, share // 128, 128)


def body(queries, pool_cache, new_blocks, w_uv, owners, slots, prefix_len, new_len, dest):
    own = lax.axis_index("pool") * REQ_DEV
    sizes = tuple(lax.axis_size(name) for name in ("groups", "pool", "head", "sub"))
    if sizes == (1, 16, 2, 1):
        gathered, arrived, fresh = gather_pool(pool_cache, new_blocks, dest[:, 0], new_len)
        gathered = gathered.reshape(-1, PACK, 128)
    else:
        gathered = lax.all_gather(pack_blocks(pool_cache), "pool", axis=0, tiled=True)
        fresh = pack_blocks(new_blocks)
        leaving = decode_rows(new_blocks, new_len, dest, own)
        gathered, leaving = lax.optimization_barrier((gathered, leaving))
        arrived = lax.all_to_all(leaving, "pool", split_axis=0, concat_axis=0, tiled=True)
    attn_out = attend(queries, gathered, fresh, w_uv, owners[:, :, 0].T, slots.T, prefix_len, new_len)
    decode_cache = arrived.reshape(arrived.shape[0], -1)
    return attn_out, decode_cache


def solution(mesh):
    placed = (
        P(("groups", "pool"), ("head", "sub")),
        P(("groups", "pool"), None),
        P(("groups", "pool"), None),
        P(("head", "sub"), None, None),
        P("groups", None, None),
        P("groups", None),
        P("groups"),
        P("groups"),
        P("groups", None),
    )
    return jax.shard_map(
        body,
        mesh=mesh,
        in_specs=placed,
        out_specs=(P(("groups", "pool"), ("head", "sub")), P(("groups", "pool"), ("head", "sub"))),
        check_vma=False,
    )
```

```python
import functools
import math

import jax
import jax.numpy as jnp
from jax import lax
from jax.experimental import pallas as pl
from jax.experimental.pallas import tpu as pltpu
from jax.sharding import PartitionSpec as P

KVL = 512
LAT = 576
VH = 128
BLK = 64
C = 64
MAXB = 8
POOL_DEV = 4
REQ_DEV = 4
WIN = 640
KEYS = (MAXB + 1) * BLK
TOK = 32
PACK = BLK * LAT // 128
TILES = KVL // 128

EXP_SCALE = 192.0 ** -0.5 * math.log2(math.e)
FAR_BELOW = -1e30


def attend_kernel(
    owners, slots, prefix_len, new_len,
    queries, gathered, fresh, w_uv, out,
    q_buf, key_buf, w_buf, keys_t, keys_v, rope, latent, q_sem, key_sem, fresh_sem, w_sem,
):
    heads = w_uv.shape[0]
    pairs = heads // 2
    first = lax.axis_index("pool") * REQ_DEV

    def q_copy(r):
        return pltpu.make_async_copy(
            queries.at[pl.ds(r * C, C)], q_buf.at[pl.ds(r * C, C)], q_sem.at[r]
        )

    def key_copy(r, k):
        row = owners[k, first + r] * POOL_DEV + slots[k, first + r]
        return pltpu.make_async_copy(
            gathered.at[row], key_buf.at[r, k + 1], key_sem.at[r, k]
        )

    def fresh_copy(r):
        return pltpu.make_async_copy(
            fresh.at[r], key_buf.at[r, 0], fresh_sem.at[r]
        )

    w_copy = pltpu.make_async_copy(w_uv, w_buf, w_sem)
    for r in range(REQ_DEV):
        fresh_copy(r).start()
        for k in range(MAXB):
            key_copy(r, k).start()
        q_copy(r).start()
    w_copy.start()

    keys_t[...] = jnp.zeros_like(keys_t)
    keys_v[pl.ds(KEYS, WIN - KEYS), :] = jnp.zeros((WIN - KEYS, KVL), jnp.bfloat16)

    def build(r, width):
        count = min(width, KEYS)
        for k in range(count // BLK):
            for j in range(TILES):
                keys_v[pl.ds(k * BLK, BLK), pl.ds(j * 128, 128)] = key_buf[r, k, pl.ds(j * BLK, BLK), :]
            tail = key_buf[r, k, pl.ds(TILES * BLK, BLK // 2), :]
            rope[pl.ds(k * BLK, BLK // 2), :] = tail[:, :LAT - KVL]
            rope[pl.ds(k * BLK + BLK // 2, BLK // 2), :] = tail[:, LAT - KVL:]
        flipped = keys_v[pl.ds(0, count), :].T
        keys_t[0, pl.ds(0, KVL), pl.ds(0, count)] = flipped
        keys_t[1, pl.ds(WIN - LAT, KVL), pl.ds(0, count)] = flipped
        flipped = rope[pl.ds(0, count), :].T
        keys_t[0, pl.ds(KVL, LAT - KVL), pl.ds(0, count)] = flipped
        keys_t[1, pl.ds(WIN - LAT + KVL, LAT - KVL), pl.ds(0, count)] = flipped

    def run(r, width, plen, nlen):
        build(r, width)

        def chunk(i, carry):
            tok = pl.multiple_of(i * TOK, TOK)
            row = pl.multiple_of(r * C + tok, TOK)
            col = lax.broadcasted_iota(jnp.int32, (TOK, width), 1)
            pos = lax.broadcasted_iota(jnp.int32, (TOK, width), 0) + tok
            last = jnp.where(col < BLK, pos, plen + BLK - 1)
            slot = col % BLK
            token = col - slot + 2 * (slot % (BLK // 2)) + slot // (BLK // 2)
            bias = jnp.where(token <= last, 0.0, FAR_BELOW)
            for parity in range(2):
                shift = parity * KVL
                q = jnp.concatenate(
                    [q_buf[pl.ds(row, TOK), pl.ds(g * 2 * LAT + shift, WIN)] for g in range(pairs)], axis=0
                )
                s = jnp.dot(q, keys_t[parity, :, :width], preferred_element_type=jnp.float32)
                s = (s.reshape(pairs, TOK, width) + bias[None]).reshape(pairs * TOK, width)
                top = jnp.max(s, axis=1, keepdims=True)
                p = jnp.exp2((s - top) * EXP_SCALE)
                total = jnp.sum(p, axis=1, keepdims=True)
                o = jnp.dot(p.astype(jnp.bfloat16), keys_v[:width], preferred_element_type=jnp.float32)
                o = (o * (1.0 / total)).astype(jnp.bfloat16)
                for g in range(pairs):
                    latent[2 * g + parity, pl.ds(row, TOK), :] = o[g * TOK:(g + 1) * TOK]
            return carry

        lax.fori_loop(0, (nlen + TOK - 1) // TOK, chunk, 0)

    def request(r, carry):
        plen = prefix_len[first + r]
        nlen = new_len[first + r]
        fresh_copy(r).wait()
        for k in range(MAXB):
            key_copy(r, k).wait()
        q_copy(r).wait()
        pl.when(plen <= 192)(lambda: run(r, 256, plen, nlen))
        pl.when((plen > 192) & (plen <= 448))(lambda: run(r, 512, plen, nlen))
        pl.when(plen > 448)(lambda: run(r, WIN, plen, nlen))
        return carry

    lax.fori_loop(0, REQ_DEV, request, 0)
    w_copy.wait()

    rows = REQ_DEV * C
    at = lax.broadcasted_iota(jnp.int32, (rows, VH), 0)
    live = jnp.zeros((rows, VH), jnp.int32)
    for r in range(REQ_DEV):
        live = jnp.where((at >= r * C) & (at < r * C + new_len[first + r]), 1, live)

    def project(h, carry):
        value = jnp.dot(latent[h], w_buf[h], preferred_element_type=jnp.float32)
        out[:, pl.ds(pl.multiple_of(h * VH, VH), VH)] = jnp.where(live == 1, value, 0.0).astype(out.dtype)
        return carry

    lax.fori_loop(0, heads, project, 0, unroll=4)


def attend(queries, gathered, fresh, w_uv, owners, slots, prefix_len, new_len):
    heads = w_uv.shape[0]
    rows = REQ_DEV * C
    flops = 2 * rows * heads * (KEYS * (LAT + KVL) + KVL * VH)
    return pl.pallas_call(
        attend_kernel,
        grid_spec=pltpu.PrefetchScalarGridSpec(
            num_scalar_prefetch=4,
            grid=(1,),
            in_specs=[pl.BlockSpec(memory_space=pl.ANY)] * 4,
            out_specs=pl.BlockSpec((rows, heads * VH), lambda i, *_: (0, 0)),
            scratch_shapes=[
                pltpu.VMEM((rows, heads * LAT), jnp.bfloat16),
                pltpu.VMEM((REQ_DEV, MAXB + 1, PACK, 128), jnp.bfloat16),
                pltpu.VMEM(w_uv.shape, jnp.bfloat16),
                pltpu.VMEM((2, WIN, WIN), jnp.bfloat16),
                pltpu.VMEM((WIN, KVL), jnp.bfloat16),
                pltpu.VMEM((KEYS, LAT - KVL), jnp.bfloat16),
                pltpu.VMEM((heads, rows, KVL), jnp.bfloat16),
                pltpu.SemaphoreType.DMA((REQ_DEV,)),
                pltpu.SemaphoreType.DMA((REQ_DEV, MAXB)),
                pltpu.SemaphoreType.DMA((REQ_DEV,)),
                pltpu.SemaphoreType.DMA,
            ],
        ),
        out_shape=jax.ShapeDtypeStruct((rows, heads * VH), jnp.bfloat16),
        compiler_params=pltpu.CompilerParams(vmem_limit_bytes=56 * 1024 * 1024),
        cost_estimate=pl.CostEstimate(flops=flops, bytes_accessed=queries.size * 2, transcendentals=rows * heads * KEYS),
        name="attend",
    )(owners, slots, prefix_len, new_len, queries, gathered, fresh, w_uv)


def gather_kernel(
    goes, lens, pool, fresh, out, decode, fresh_out, packed, raw, leaving, own_sem, stay_sem, push_send, push_recv,
    z_send, z_recv, y_send, y_recv, x_send, x_recv, far_send, far_recv, c_send, c_recv,
):
    me = lax.axis_index("pool")
    x = lax.axis_index("head")
    z, y, c = me // 4, (me // 2) % 2, me % 2
    lane = lax.broadcasted_iota(jnp.int32, (BLK // 2, 128), 1)

    def spread(ref):
        def step(i, carry):
            at = pl.multiple_of(i * 256, 256)
            both = jnp.concatenate([ref[:, pl.ds(at, 128)], ref[:, pl.ds(at + 128, 128)]], axis=0)
            raw[pl.ds(pl.multiple_of(i * 8, 8), 8), :] = both.astype(jnp.float32)
            return carry

        lax.fori_loop(0, PACK // 2, step, 0, unroll=8)

    def pack(ref):
        for b in range(POOL_DEV):
            nine = [raw[pl.ds(POOL_DEV * j + b, BLK // 2, stride=9 * POOL_DEV), :] for j in range(9)]
            turned = [pltpu.roll(row, 64, 1) for row in nine[4:]]
            for j in range(TILES):
                odd = jnp.where(lane < 64, turned[j], turned[j + 1])
                ref[b, pl.ds(j * BLK, BLK), :] = jnp.concatenate([nine[j], odd], axis=0).astype(ref.dtype)
            ref[b, pl.ds(TILES * BLK, BLK // 2), :] = jnp.where(lane < 64, nine[4], nine[8]).astype(ref.dtype)

    def group(zz, yy, cc):
        return zz * 4 + yy * 2 + cc

    below, above = {"pool": me - 4}, {"pool": me + 4}
    beside, across, sibling = {"pool": group(z, 1 - y, c)}, {"head": 1 - x}, {"pool": group(z, y, 1 - c)}

    barrier = pltpu.get_barrier_semaphore()

    def greet(device):
        pl.semaphore_signal(barrier, inc=1, device_id=device, device_id_type=pl.DeviceIdType.MESH)

    peers = decode.shape[0]
    greet(across)
    for n in range(1, peers):
        greet({"pool": (me + n) % peers})

    spread(pool)
    pack(packed)

    inner = (z > 0) & (z < 3)
    end = jnp.logical_not(inner)
    pl.semaphore_wait(barrier, peers)

    def real(l):
        return l + x * (3 - 2 * l)

    def copy(g, l, send, recv, device, own=False):
        src = packed.at[real(l)] if own else out.at[g, real(l)]
        return pltpu.make_async_remote_copy(
            src_ref=src, dst_ref=out.at[g, real(l)], send_sem=send, recv_sem=recv,
            device_id=device, device_id_type=pl.DeviceIdType.MESH,
        )

    def z_copy(zz, l, up, own=False):
        return copy(group(zz, y, c), l, z_send.at[up, zz, l], z_recv.at[zz, l], above if up else below, own)

    def y_copy(zz, yy, l, own=False):
        return copy(group(zz, yy, c), l, y_send.at[zz, l], y_recv.at[zz, l], beside, own)

    def x_copy(zz, l, came=False):
        return copy(group(zz, 1 - y, c), 3 - l if came else l, x_send.at[zz, l], x_recv.at[zz, l], across)

    def far_copy(l, came=False):
        return copy(group(3 - z, y, c), 3 - l if came else l, far_send.at[l], far_recv.at[l], across)

    def c_copy(zz, yy, cc, l, own=False):
        return copy(group(zz, yy, cc), l, c_send.at[zz, yy, l], c_recv.at[zz, yy, l], sibling, own)

    def each(distance, act):
        if distance == 0:
            act(z, None)
        else:
            pl.when(z + distance <= 3)(lambda: act(z + distance, False))
            pl.when(z - distance >= 0)(lambda: act(z - distance, True))

    def z_round(distance, part):
        own = distance == 0
        for l in part:
            def line(zz, up, l=l):
                if not own:
                    z_copy(zz, l, up).wait_recv()
                if distance < 2 or l < 2:
                    if up is None or up:
                        pl.when(z < 3)(lambda: z_copy(zz, l, 1, own).start())
                    if up is None or not up:
                        pl.when(z > 0)(lambda: z_copy(zz, l, 0, own).start())
                if l < 2:
                    y_copy(zz, y, l, own).start()
                if distance == 3:
                    far_copy(l).start()
                c_copy(zz, y, c, l, own).start()

            each(distance, line)

    def y_round(distance):
        for l in range(2):
            def side(zz, up, l=l):
                y_copy(zz, 1 - y, l).wait_recv()
                x_copy(zz, l).start()
                c_copy(zz, 1 - y, c, l).start()

            each(distance, side)

    def x_round(distance):
        for l in range(2):
            def side(zz, up, l=l):
                x_copy(zz, l, True).wait_recv()
                c_copy(zz, 1 - y, c, 3 - l).start()

            each(distance, side)

    early, late = (0, 1), (2, 3)
    z_round(0, early)
    own_copy = pltpu.make_async_copy(packed, out.at[me], own_sem)
    own_copy.start()

    spread(fresh)
    pack(fresh_out)
    span = leaving.shape[1]
    start = x * span
    place = (lax.broadcasted_iota(jnp.int32, (span, 128), 0) + start) * 128 + lax.broadcasted_iota(jnp.int32, (span, 128), 1)
    rows = []
    for r in range(REQ_DEV):
        value = raw[pl.ds(start * REQ_DEV + r, span, stride=REQ_DEV), :]
        target = jnp.full((span, 128), goes[me * REQ_DEV + r], jnp.int32)
        rows.append((target, jnp.where(place < lens[me * REQ_DEV + r] * LAT, value, 0.0)))
    for n in range(leaving.shape[0]):
        row = jnp.zeros((span, 128), jnp.float32)
        for target, value in rows:
            row = jnp.where(target == n, value, row)
        leaving[n] = row.astype(leaving.dtype)

    def push(n):
        peer = (me + n) % peers
        return pltpu.make_async_remote_copy(
            src_ref=leaving.at[peer], dst_ref=decode.at[me], send_sem=push_send.at[peer], recv_sem=push_recv.at[me],
            device_id={"pool": peer}, device_id_type=pl.DeviceIdType.MESH,
        )

    def pushed(n):
        peer = (me + n) % peers
        return pltpu.make_async_remote_copy(
            src_ref=leaving.at[peer], dst_ref=decode.at[peer], send_sem=push_send.at[peer], recv_sem=push_recv.at[peer],
            device_id={"pool": peer}, device_id_type=pl.DeviceIdType.MESH,
        )

    stay = pltpu.make_async_copy(leaving.at[me], decode.at[me], stay_sem)
    stay.start()

    z_round(1, early)
    y_round(0)
    z_round(0, late)
    z_round(2, early)
    x_round(0)
    y_round(1)
    z_round(3, early)
    z_round(1, late)
    for n in range(1, peers):
        push(n).start()
    x_round(1)
    y_round(2)
    x_round(2)
    y_round(3)
    z_round(2, late)

    def far_round():
        for l in range(2):
            far_copy(l, True).wait_recv()
            c_copy(3 - z, y, c, 3 - l).start()

    pl.when(end)(far_round)
    x_round(3)

    own_copy.wait()
    stay.wait()
    for n in range(1, peers):
        pushed(n).wait_recv()
        push(n).wait_send()
    for zz in range(4):
        for yy in range(2):
            for l in range(4):
                c_copy(zz, yy, 1 - c, l).wait_recv()

    for zz in range(4):
        for l in range(4):
            reach = 3 if l < 2 else 1
            pl.when((z < 3) & (zz <= z) & (z - zz <= reach))(lambda zz=zz, l=l: z_copy(zz, l, 1).wait_send())
            pl.when((z > 0) & (zz >= z) & (zz - z <= reach))(lambda zz=zz, l=l: z_copy(zz, l, 0).wait_send())
            for yy in range(2):
                c_copy(zz, yy, c, l).wait_send()
        for l in range(2):
            y_copy(zz, y, l).wait_send()
            x_copy(zz, l).wait_send()

    def far_sent():
        for l in range(2):
            far_copy(l).wait_send()

    pl.when(end)(far_sent)


def gather_pool(pool_cache, new_blocks, dest, new_len):
    pool_count = lax.axis_size("pool")
    span = PACK // lax.axis_size("head")
    dma = pltpu.SemaphoreType.DMA
    kind = pool_cache.dtype
    vmem, smem = pl.BlockSpec(memory_space=pltpu.VMEM), pl.BlockSpec(memory_space=pltpu.SMEM)
    return pl.pallas_call(
        gather_kernel,
        out_shape=(
            jax.ShapeDtypeStruct((pool_count, POOL_DEV, PACK, 128), kind),
            jax.ShapeDtypeStruct((pool_count, span, 128), kind),
            jax.ShapeDtypeStruct((REQ_DEV, PACK, 128), kind),
        ),
        in_specs=[smem, smem, vmem, vmem],
        out_specs=(pl.BlockSpec(memory_space=pl.ANY), pl.BlockSpec(memory_space=pl.ANY), vmem),
        scratch_shapes=[
            pltpu.VMEM((POOL_DEV, PACK, 128), kind), pltpu.VMEM((POOL_DEV * PACK, 128), jnp.float32),
            pltpu.VMEM((pool_count, span, 128), kind), dma, dma, dma((pool_count,)), dma((pool_count,)),
            dma((2, 4, 4)), dma((4, 4)), dma((4, 2)), dma((4, 2)), dma((4, 2)), dma((4, 2)), dma((2,)), dma((2,)),
            dma((4, 2, 4)), dma((4, 2, 4)),
        ],
        compiler_params=pltpu.CompilerParams(
            collective_id=0, has_side_effects=True, vmem_limit_bytes=56 * 1024 * 1024
        ),
        name="gather_pool",
    )(dest, new_len, pool_cache, new_blocks)


def pack_blocks(blocks):
    blocks = blocks.reshape(-1, BLK // 2, 2, LAT).transpose(0, 2, 1, 3).reshape(-1, BLK, LAT)
    lanes = blocks[:, :, :KVL].reshape(-1, BLK, TILES, 128).transpose(0, 2, 1, 3).reshape(-1, TILES * BLK, 128)
    tail = jnp.concatenate([blocks[:, :BLK // 2, KVL:], blocks[:, BLK // 2:, KVL:]], axis=2)
    return jnp.concatenate([lanes, tail], axis=1)


def decode_rows(new_blocks, new_len, dest, own):
    pool_count = lax.axis_size("pool")
    share = new_blocks.shape[1] // lax.axis_size(("head", "sub"))
    start = lax.axis_index(("head", "sub")) * share
    part = lax.dynamic_slice_in_dim(new_blocks, start, share, 1)
    tok = (jnp.arange(share, dtype=jnp.int32) + start) // LAT
    lens = lax.dynamic_slice_in_dim(new_len, own, REQ_DEV, 0)
    goes = lax.dynamic_slice_in_dim(dest[:, 0], own, REQ_DEV, 0)
    part = jnp.where(tok[None, :] < lens[:, None], part, 0)
    rows = jnp.zeros((pool_count, share), new_blocks.dtype)
    for r in range(REQ_DEV):
        rows = jnp.where((goes[r] == jnp.arange(pool_count))[:, None], part[r][None, :], rows)
    return rows.reshape(pool_count, share // 128, 128)


def body(queries, pool_cache, new_blocks, w_uv, owners, slots, prefix_len, new_len, dest):
    own = lax.axis_index("pool") * REQ_DEV
    sizes = tuple(lax.axis_size(name) for name in ("groups", "pool", "head", "sub"))
    if sizes == (1, 16, 2, 1):
        gathered, arrived, fresh = gather_pool(pool_cache, new_blocks, dest[:, 0], new_len)
        gathered = gathered.reshape(-1, PACK, 128)
    else:
        gathered = lax.all_gather(pack_blocks(pool_cache), "pool", axis=0, tiled=True)
        fresh = pack_blocks(new_blocks)
        leaving = decode_rows(new_blocks, new_len, dest, own)
        gathered, leaving = lax.optimization_barrier((gathered, leaving))
        arrived = lax.all_to_all(leaving, "pool", split_axis=0, concat_axis=0, tiled=True)
    attn_out = attend(queries, gathered, fresh, w_uv, owners[:, :, 0].T, slots.T, prefix_len, new_len)
    decode_cache = arrived.reshape(arrived.shape[0], -1)
    return attn_out, decode_cache


def solution(mesh):
    placed = (
        P(("groups", "pool"), ("head", "sub")),
        P(("groups", "pool"), None),
        P(("groups", "pool"), None),
        P(("head", "sub"), None, None),
        P("groups", None, None),
        P("groups", None),
        P("groups"),
        P("groups"),
        P("groups", None),
    )
    return jax.shard_map(
        body,
        mesh=mesh,
        in_specs=placed,
        out_specs=(P(("groups", "pool"), ("head", "sub")), P(("groups", "pool"), ("head", "sub"))),
        check_vma=False,
    )
```
